32 devices in a mesh: slab: 8 (over z, x), layer: 4 (over y, core).
Axes of the slice: x: 2, y: 2, z: 4, core: 2. Of those that a mesh axis runs over, the one named last changes fastest.
Arguments:
- adjoint_source: float32 [4, 128, 4096], P('layer', 'slab')
- conductivity: float32 [4, 128, 4096], P('layer', 'slab'), may hold values from 0.3 to 3
- tile_owner: int32 [1, 32], replicated, may hold values from 0 to 7, as said below
Outputs:
- adjoint: float32 [4, 128, 4096], P('layer', 'slab')
- owned_grad: float32 [32, 128, 128], P('slab', 'layer')
The draws below stay inside these ranges and needn't reach their ends.
Inputs may be any that keep to these rules, and one draw needn't show every extreme that they name: `tile_owner`: every owner holds exactly 4 tiles, and in every row of tiles each owner holds at most 4 tile; in every row some owner holds 4 tile.
All inputs are finite; a program needn't handle non-finite values.
Results may differ from the reference program's by a relative error of at most 0.0003.
Values sent between devices are 32-bit elements; how exact they have to be, the bound alone decides.
A program may use at most 64 MiB of HBM per device.

```python
import math
import jax
import jax.numpy as jnp

TILE = 128
TC = 32
ITERS = 3
NX = 128
NY = 4096
NL = 4
TR = 1
N_SLAB = 8


def draw_adjoint_source(key, part):
    key = jax.random.fold_in(key, 11)
    layer_pos = jnp.arange(NL, dtype=jnp.float32)[:, None, None] / max(NL - 1, 1)
    row_pos = jnp.arange(NX, dtype=jnp.float32)[None, :, None] / max(NX - 1, 1)
    rough = jax.random.normal(key, (NL, NX, NY), jnp.float32)
    growth = jnp.power(3.0, row_pos) * jnp.power(3.0, layer_pos)
    return (growth * rough).astype(jnp.float32)


def draw_tile_owner(key, part):
    key = jax.random.fold_in(key, 23)
    first_key, second_key = jax.random.split(key)
    relabel = jax.random.permutation(first_key, N_SLAB)

    def shuffle_row(row_key):
        return jax.random.permutation(row_key, TC)
    columns = jax.vmap(shuffle_row)(jax.random.split(second_key, TR))
    position = (jnp.arange(TR, dtype=jnp.int32)[:, None] * TC + columns.astype(jnp.int32)) % N_SLAB
    return relabel[position].astype(jnp.int32)


def block_scale(rng, extent, shards, least, top_value):
    loudness = 1.0
    for dim, blocks in shards:
        heights = jax.random.uniform(jax.random.fold_in(jax.random.fold_in(rng, 6), dim), (blocks,), jnp.float32, least / len(shards), top_value / len(shards))
        loudness = loudness * jnp.repeat(jnp.exp(heights), extent[dim] // blocks).reshape((-1,) + (1,) * (len(extent) - 1 - dim))
    return loudness


def setup_inputs(seed: int = 0) -> dict:
    seeds = jax.random.split(jax.random.key(seed), 4)
    adjoint_source = draw_adjoint_source(jax.random.fold_in(seeds[3], 71), 0)
    conductivity = jnp.clip(jnp.exp(math.log(3.0) - 2.3025851 * jax.random.uniform(seeds[1], (NL, NX, NY), jnp.float32) ** block_scale(seeds[1], (NL, NX, NY), ((0, 4), (1, 8)), -0.2, 0.2)), 0.3, 3.0)
    tile_owner = draw_tile_owner(jax.random.fold_in(seeds[3], 71), 0)
    return {"adjoint_source": adjoint_source, "conductivity": conductivity, "tile_owner": tile_owner}


def neighbours(padded):
    return [padded[2:, 1:-1, 1:-1], padded[:-2, 1:-1, 1:-1],
            padded[1:-1, 2:, 1:-1], padded[1:-1, :-2, 1:-1],
            padded[1:-1, 1:-1, 2:], padded[1:-1, 1:-1, :-2]]


def apply_operator(field, conductivity):
    result = jnp.zeros_like(field)
    cond_near = neighbours(jnp.pad(conductivity, 1))
    field_near = neighbours(jnp.pad(field, 1))
    for near_cond, near_field in zip(cond_near, field_near):
        result = result + 0.5 * (conductivity + near_cond) * (field - near_field)
    return result


def reference(adjoint_source, conductivity, tile_owner):
    diagonal = jnp.zeros_like(conductivity)
    for near_cond in neighbours(jnp.pad(conductivity, 1)):
        diagonal = diagonal + 0.5 * (conductivity + near_cond)
    inverse = 1.0 / diagonal
    solution = jnp.zeros_like(adjoint_source)
    residual = adjoint_source
    precond = inverse * residual
    direction = precond
    inner_now = jnp.sum(residual * precond)
    for iteration in range(ITERS):
        product_field = apply_operator(direction, conductivity)
        step_size = inner_now / jnp.sum(direction * product_field)
        solution = solution + step_size * direction
        residual = residual - step_size * product_field
        if iteration + 1 < ITERS:
            precond = inverse * residual
            inner_next = jnp.sum(residual * precond)
            direction = precond + (inner_next / inner_now) * direction
            inner_now = inner_next
    gradient = jnp.sum(solution, axis=0)
    tile_blocks = gradient.reshape(TR, TILE, TC, TILE).transpose(0, 2, 3, 1).reshape(TR * TC, TILE, TILE)
    tile_order = jnp.argsort(tile_owner.reshape(-1), stable=True)
    return solution, tile_blocks[tile_order]
```

```python
import functools

import jax
import jax.numpy as jnp
from jax import lax
from jax.experimental import pallas as pl
from jax.experimental.pallas import tpu as pltpu
from jax.sharding import PartitionSpec as P

TILE = 128
ITERS = 3
CHUNKS = 4
PAD = 128
MESH = pl.DeviceIdType.MESH


def fold(value):
    rows = sum(value[i : i + 8] for i in range(0, value.shape[0], 8))
    return sum(rows[:, i : i + 128] for i in range(0, value.shape[1], 128))


def cg_coefficients(mu):
    def inner(a, b):
        total = None
        for k in range(len(a) + len(b) - 1):
            coef = None
            for i in range(len(a)):
                if 0 <= k - i < len(b):
                    term = a[i] * b[k - i]
                    coef = term if coef is None else coef + term
            total = coef * mu[k] if total is None else total + coef * mu[k]
        return total

    def axpy(a, s, b):
        out = []
        for i in range(max(len(a), len(b))):
            if i >= len(b):
                out.append(a[i])
            elif i >= len(a):
                out.append(s * b[i])
            else:
                out.append(a[i] + s * b[i])
        return out

    one = jnp.ones_like(mu[0])
    zero = jnp.zeros_like(mu[0])
    sol, res, direction, now = [zero], [one], [one], mu[0]
    for iteration in range(ITERS):
        image = axpy(direction + [zero], -one, [zero] + direction)
        step = now / inner(direction, image)
        sol = axpy(sol, step, direction)
        if iteration + 1 < ITERS:
            res = axpy(res, -step, image)
            new = inner(res, res)
            direction = axpy(res, new / now, direction)
            now = new
    return sol


def kernel(
    n_slab,
    n_layer,
    src_ref,
    cond_ref,
    owner_ref,
    x_out,
    g_out,
    fields,
    coefs,
    inv_ref,
    layer_halo,
    row_send,
    row_recv,
    red_layer,
    red_slab,
    x_buf,
    x_tiles,
    strip_send,
    strip_recv,
    tile_send,
    tile_recv,
    table,
    halo_ssem,
    halo_rsem,
    red_ssem,
    red_rsem,
    strip_ssem,
    strip_rsem,
    tile_ssem,
    tile_rsem,
    out_sem,
):
    slab = lax.axis_index("slab")
    layer = lax.axis_index("layer")
    rows, cols = src_ref.shape[1], src_ref.shape[2]
    width = cols // CHUNKS
    top, bottom = 8, 8 + rows
    tile_rows, tiles_across = owner_ref.shape
    strip = TILE // n_layer
    capacity = max(1, tiles_across // n_slab)
    owned_count = g_out.shape[0]
    per_tile = TILE // rows

    def peers(axis, me, count):
        return [(d, {axis: lax.rem(me + d, count)}, lax.rem(me + count - d, count)) for d in range(1, count)]

    layer_peers = peers("layer", layer, n_layer)
    slab_peers = peers("slab", slab, n_slab)

    barrier = pltpu.get_barrier_semaphore()
    for _, device, _ in layer_peers + slab_peers:
        pl.semaphore_signal(barrier, inc=1, device_id=device, device_id_type=MESH)

    for s in range(4):
        fields[s, :, 0:PAD] = jnp.zeros((rows + 16, PAD), jnp.float32)
        fields[s, :, PAD + cols :] = jnp.zeros((rows + 16, PAD), jnp.float32)
    for d, axis_end in enumerate((layer == 0, layer == n_layer - 1)):

        @pl.when(axis_end)
        def _():
            for s in range(4):
                layer_halo[s, d] = jnp.zeros((rows, cols), jnp.float32)

    for d, axis_end in enumerate((slab == 0, slab == n_slab - 1)):

        @pl.when(axis_end)
        def _():
            for s in range(4):
                for j in range(CHUNKS):
                    row_recv[s, d, j] = jnp.zeros((1, width), jnp.float32)

    sends_to = (layer < n_layer - 1, layer > 0, slab < n_slab - 1, slab > 0)
    gets_from = (layer > 0, layer < n_layer - 1, slab > 0, slab < n_slab - 1)
    target = (
        {"layer": lax.rem(layer + 1, n_layer)},
        {"layer": lax.rem(layer + n_layer - 1, n_layer)},
        {"slab": lax.rem(slab + 1, n_slab)},
        {"slab": lax.rem(slab + n_slab - 1, n_slab)},
    )

    def used(stage, direction, j):
        if stage < 3:
            return True
        if direction == 0:
            return j < CHUNKS // 2
        if direction == 1:
            return j >= CHUNKS // 2
        return direction == 2

    def halo_copy(stage, direction, j):
        span = pl.ds(j * width, width)
        if direction < 2:
            source = fields.at[stage, pl.ds(top, rows), pl.ds(PAD + j * width, width)]
            dest = layer_halo.at[stage, direction, :, span]
        else:
            source = row_send.at[stage, direction - 2, j]
            dest = row_recv.at[stage, direction - 2, j]
        return pltpu.make_async_remote_copy(
            src_ref=source,
            dst_ref=dest,
            send_sem=halo_ssem.at[stage, direction, j],
            recv_sem=halo_rsem.at[stage, direction, j],
            device_id=target[direction],
            device_id_type=MESH,
        )

    def put_field(stage, j, value):
        fields[stage, top:bottom, PAD + j * width : PAD + (j + 1) * width] = value
        row_send[stage, 0, j] = value[rows - 1 : rows]
        row_send[stage, 1, j] = value[0:1]

    def send_field(stage, j):
        for direction in range(4):
            if used(stage, direction, j):

                @pl.when(sends_to[direction])
                def _():
                    halo_copy(stage, direction, j).start()

    def get_halo(stage, j):
        for direction in range(4):
            if used(stage, direction, j):

                @pl.when(gets_from[direction])
                def _():
                    halo_copy(stage, direction, j).wait_recv()

        span = slice(PAD + j * width, PAD + (j + 1) * width)
        fields[stage, top - 1 : top, span] = row_recv[stage, 0, j]
        if stage < 3:
            fields[stage, bottom : bottom + 1, span] = row_recv[stage, 1, j]

    def near(stage, j, which):
        c0 = j * width
        if which == "west":
            ext = fields[stage, top:bottom, c0 : c0 + width + 2 * PAD]
            return pltpu.roll(ext, 1, 1)[:, PAD : PAD + width]
        if which == "east":
            ext = fields[stage, top:bottom, c0 : c0 + width + 2 * PAD]
            return pltpu.roll(ext, width + 2 * PAD - 1, 1)[:, PAD : PAD + width]
        span = slice(PAD + c0, PAD + c0 + width)
        if which == "north":
            return fields[stage, top - 1 : bottom - 1, span]
        if which == "south":
            return fields[stage, top + 1 : bottom + 1, span]
        return layer_halo[stage, 0 if which == "below" else 1, :, c0 : c0 + width]

    names = ("west", "east", "north", "south", "below", "above")

    def here(stage, j):
        return fields[stage, top:bottom, PAD + j * width : PAD + (j + 1) * width]

    for j in range(CHUNKS):
        put_field(0, j, cond_ref[0, :, j * width : (j + 1) * width])
    pl.semaphore_wait(barrier, n_layer + n_slab - 2)
    for j in range(CHUNKS):
        send_field(0, j)

    my_row = slab // per_tile

    def list_tiles(owner, carry):
        packed = jnp.int32(0)
        for t in range(tiles_across):
            packed = jnp.where(owner_ref[my_row, t] == owner, packed * 256 + t, packed)
        table[owner] = packed
        return carry

    lax.fori_loop(0, n_slab, list_tiles, 0)

    moments = [jnp.zeros((8, 128), jnp.float32) for _ in range(6)]
    for j in range(CHUNKS):
        get_halo(0, j)
        span = slice(j * width, (j + 1) * width)
        cond = here(0, j)
        diagonal = None
        for i, name in enumerate(names):
            face = cond + near(0, j, name)
            coefs[i, :, span] = face
            diagonal = face if diagonal is None else diagonal + face
        inverse = 1.0 / diagonal
        inv_ref[:, span] = inverse
        source = src_ref[0, :, span]
        field = source * inverse
        put_field(1, j, field)
        send_field(1, j)
        moments[0] = moments[0] + fold(field * source)
    for stage in (1, 2):
        for j in range(CHUNKS):
            get_halo(stage, j)
            span = slice(j * width, (j + 1) * width)
            image = None
            for i, name in enumerate(names):
                term = coefs[i, :, span] * near(stage, j, name)
                image = term if image is None else image + term
            field = inv_ref[:, span] * image
            put_field(stage + 1, j, field)
            send_field(stage + 1, j)
            moments[2 * stage - 1] = moments[2 * stage - 1] + fold(here(stage, j) * image)
            moments[2 * stage] = moments[2 * stage] + fold(field * image)
    for j in range(CHUNKS):
        get_halo(3, j)
        span = slice(j * width, (j + 1) * width)
        side = "below" if j < CHUNKS // 2 else "above"
        image = None
        for name in ("west", "north", side):
            term = coefs[names.index(name), :, span] * near(3, j, name)
            image = term if image is None else image + term
        moments[5] = moments[5] + fold(here(3, j) * image)
    moments[5] = 2.0 * moments[5]

    def exchange(peer_list, me, send_of, recv_buf, ssem, rsem):
        copies = []
        for d, device, _ in peer_list:
            copy = pltpu.make_async_remote_copy(
                src_ref=send_of(d, device),
                dst_ref=recv_buf.at[me],
                send_sem=ssem.at[d],
                recv_sem=rsem.at[d],
                device_id=device,
                device_id_type=MESH,
            )
            copy.start()
            copies.append(copy)
        return copies

    sums = [jnp.sum(m, axis=0, keepdims=True) for m in moments]
    red_layer[layer] = jnp.concatenate(sums + [jnp.zeros((2, 128), jnp.float32)], axis=0)
    first = exchange(layer_peers, layer, lambda d, device: red_layer.at[layer], red_layer, red_ssem.at[0], red_rsem.at[0])
    for copy in first:
        copy.wait_recv()
    red_slab[slab] = sum(red_layer[i] for i in range(n_layer))
    second = exchange(slab_peers, slab, lambda d, device: red_slab.at[slab], red_slab, red_ssem.at[1], red_rsem.at[1])
    for copy in second:
        copy.wait_recv()
    total = jnp.sum(sum(red_slab[i] for i in range(n_slab)), axis=1, keepdims=True)
    scales = [2.0 * c for c in cg_coefficients([total[k : k + 1] for k in range(6)])]

    for j in range(CHUNKS):
        value = scales[0] * here(1, j) + scales[1] * here(2, j) + scales[2] * here(3, j)
        x_buf[:, j * width : (j + 1) * width] = value
        for t in range(width // TILE):
            x_tiles[j * (width // TILE) + t] = value[:, t * TILE : (t + 1) * TILE]
    x_copy = pltpu.make_async_copy(x_buf, x_out.at[0], out_sem)
    x_copy.start()

    lane = lax.broadcasted_iota(jnp.int32, (rows, TILE), 1) // strip

    def pack(owner, carry):
        packed = table[owner]
        pieces = [None] * n_layer
        for q in range(capacity):
            t = lax.shift_right_logical(packed, 8 * (capacity - 1 - q)) & 255
            tile = x_tiles[t]
            for target_layer in range(n_layer):
                shift = ((q - target_layer) * strip) % TILE
                moved = tile if shift == 0 else pltpu.roll(tile, shift, 1)
                old = pieces[target_layer]
                pieces[target_layer] = moved if old is None else jnp.where(lane == q, moved, old)
        for target_layer in range(n_layer):
            strip_send[target_layer, owner] = pieces[target_layer]
        return carry

    lax.fori_loop(0, n_slab, pack, 0)
    third = exchange(
        layer_peers, layer, lambda d, device: strip_send.at[device["layer"]], strip_recv, strip_ssem, strip_rsem
    )
    strip_recv[layer] = strip_send[layer]
    for copy in third:
        copy.wait_recv()
    for owner in range(n_slab):
        tile_send[owner] = sum(strip_recv[i, owner] for i in range(n_layer))
    fourth = exchange(
        slab_peers, slab, lambda d, device: tile_send.at[device["slab"]], tile_recv, tile_ssem, tile_rsem
    )
    tile_recv[slab] = tile_send[slab]
    for copy in fourth:
        copy.wait_recv()
    if tile_rows == 1:
        turned = jnp.transpose(tile_recv[...].reshape(TILE, TILE))
        for k in range(owned_count):
            g_out[k] = turned[k * strip : (k + 1) * strip]
    else:
        count = jnp.int32(0)
        picked = [jnp.int32(0)] * owned_count
        for r in range(tile_rows):
            for t in range(tiles_across):
                mine = owner_ref[r, t] == slab
                picked = [jnp.where(mine & (count == k), r, p) for k, p in enumerate(picked)]
                count = jnp.where(mine, count + 1, count)
        for k in range(owned_count):
            block = tile_recv[pl.ds(picked[k] * per_tile, per_tile)].reshape(TILE, TILE)
            g_out[k] = jnp.transpose(block)[0:strip]

    for stage in range(4):
        for j in range(CHUNKS):
            for direction in range(4):
                if used(stage, direction, j):

                    @pl.when(sends_to[direction])
                    def _():
                        halo_copy(stage, direction, j).wait_send()

    for copy in first + second + third + fourth:
        copy.wait_send()
    x_copy.wait()


def per_device(adjoint_source, conductivity, tile_owner):
    n_slab, n_layer = lax.axis_size("slab"), lax.axis_size("layer")
    depth, rows, cols = adjoint_source.shape
    owned = tile_owner.shape[0] * tile_owner.shape[1] // n_slab
    strip = TILE // n_layer
    width = cols // CHUNKS
    vmem = pl.BlockSpec(memory_space=pltpu.VMEM)
    f32 = jnp.float32
    return pl.pallas_call(
        functools.partial(kernel, n_slab, n_layer),
        out_shape=(
            jax.ShapeDtypeStruct((depth, rows, cols), f32),
            jax.ShapeDtypeStruct((owned, strip, TILE), f32),
        ),
        in_specs=[vmem, vmem, pl.BlockSpec(memory_space=pltpu.SMEM)],
        out_specs=(pl.BlockSpec(memory_space=pl.ANY), vmem),
        scratch_shapes=[
            pltpu.VMEM((4, rows + 16, cols + 2 * PAD), f32),
            pltpu.VMEM((6, rows, cols), f32),
            pltpu.VMEM((rows, cols), f32),
            pltpu.VMEM((4, 2, rows, cols), f32),
            pltpu.VMEM((4, 2, CHUNKS, 1, width), f32),
            pltpu.VMEM((4, 2, CHUNKS, 1, width), f32),
            pltpu.VMEM((n_layer, 8, 128), f32),
            pltpu.VMEM((n_slab, 8, 128), f32),
            pltpu.VMEM((rows, cols), f32),
            pltpu.VMEM((cols // TILE, rows, TILE), f32),
            pltpu.VMEM((n_layer, n_slab, rows, TILE), f32),
            pltpu.VMEM((n_layer, n_slab, rows, TILE), f32),
            pltpu.VMEM((n_slab, rows, TILE), f32),
            pltpu.VMEM((n_slab, rows, TILE), f32),
            pltpu.SMEM((n_slab,), jnp.int32),
            pltpu.SemaphoreType.DMA((4, 4, CHUNKS)),
            pltpu.SemaphoreType.DMA((4, 4, CHUNKS)),
            pltpu.SemaphoreType.DMA((2, max(n_slab, n_layer))),
            pltpu.SemaphoreType.DMA((2, max(n_slab, n_layer))),
            pltpu.SemaphoreType.DMA((n_layer,)),
            pltpu.SemaphoreType.DMA((n_layer,)),
            pltpu.SemaphoreType.DMA((n_slab,)),
            pltpu.SemaphoreType.DMA((n_slab,)),
            pltpu.SemaphoreType.DMA,
        ],
        compiler_params=pltpu.CompilerParams(
            collective_id=0, has_side_effects=True, vmem_limit_bytes=48 * 1024 * 1024
        ),
        name="stack_cg",
    )(adjoint_source, conductivity, tile_owner)


def solution(mesh):
    placed = (P("layer", "slab", None), P("layer", "slab", None), P())
    return jax.shard_map(
        per_device,
        mesh=mesh,
        in_specs=placed,
        out_specs=(P("layer", "slab", None), P("slab", "layer", None)),
        check_vma=False,
    )
```

```python
import functools

import jax
import jax.numpy as jnp
from jax import lax
from jax.experimental import pallas as pl
from jax.experimental.pallas import tpu as pltpu
from jax.sharding import PartitionSpec as P

TILE = 128
ITERS = 3
CHUNKS = 4
PAD = 128
MESH = pl.DeviceIdType.MESH


def fold(value):
    rows = sum(value[i : i + 8] for i in range(0, value.shape[0], 8))
    return sum(rows[:, i : i + 128] for i in range(0, value.shape[1], 128))


def cg_coefficients(mu):
    def inner(a, b):
        total = None
        for k in range(len(a) + len(b) - 1):
            coef = None
            for i in range(len(a)):
                if 0 <= k - i < len(b):
                    term = a[i] * b[k - i]
                    coef = term if coef is None else coef + term
            total = coef * mu[k] if total is None else total + coef * mu[k]
        return total

    def axpy(a, s, b):
        out = []
        for i in range(max(len(a), len(b))):
            if i >= len(b):
                out.append(a[i])
            elif i >= len(a):
                out.append(s * b[i])
            else:
                out.append(a[i] + s * b[i])
        return out

    one = jnp.ones_like(mu[0])
    zero = jnp.zeros_like(mu[0])
    sol, res, direction, now = [zero], [one], [one], mu[0]
    for iteration in range(ITERS):
        image = axpy(direction + [zero], -one, [zero] + direction)
        step = now / inner(direction, image)
        sol = axpy(sol, step, direction)
        if iteration + 1 < ITERS:
            res = axpy(res, -step, image)
            new = inner(res, res)
            direction = axpy(res, new / now, direction)
            now = new
    return sol


def kernel(
    n_slab,
    n_layer,
    src_hbm,
    cond_hbm,
    owner_hbm,
    x_out,
    g_out,
    src_ref,
    owner_ref,
    fields,
    coefs,
    inv_ref,
    layer_halo,
    row_send,
    row_recv,
    red_layer,
    red_slab,
    x_buf,
    x_tiles,
    tile_send,
    tile_recv,
    table,
    halo_ssem,
    halo_rsem,
    red_ssem,
    red_rsem,
    tile_ssem,
    tile_rsem,
    local_sem,
):
    slab = lax.axis_index("slab")
    layer = lax.axis_index("layer")
    rows, cols = src_ref.shape
    width = cols // CHUNKS
    top, bottom = 8, 8 + rows
    tile_rows, tiles_across = owner_ref.shape
    strip = TILE // n_layer
    capacity = max(1, tiles_across // n_slab)
    owned_count = g_out.shape[0]
    per_tile = TILE // rows

    pair, core = layer // 2, layer % 2
    n_pair = n_layer // 2

    def turn(me, d, count):
        return lax.rem(me + d, count)

    def layer_peer(d):
        return {"layer": turn(layer, d, n_layer)}

    def slab_peer(d):
        return {"slab": turn(slab, d, n_slab)}

    def tile_peer(n):
        to_pair, to_slab = turn(pair, n // n_slab, n_pair), turn(slab, n % n_slab, n_slab)
        return to_pair, to_slab, {"layer": 2 * to_pair + core, "slab": to_slab}

    def repeat(start, stop, body):
        if stop - start <= 32:
            for n in range(start, stop):
                body(n)
        else:
            lax.fori_loop(start, stop, lambda n, carry: (body(n), carry)[1], 0)

    barrier = pltpu.get_barrier_semaphore()

    def greet(device):
        pl.semaphore_signal(barrier, inc=1, device_id=device, device_id_type=MESH)

    n_greet = 0
    for d in range(1, n_layer):
        if d % 2 == 1:
            greet(layer_peer(d))
            n_greet += 1
    repeat(1, n_pair * n_slab, lambda n: greet(tile_peer(n)[2]))
    n_greet += n_pair * n_slab - 1

    cond_copy = pltpu.make_async_copy(
        cond_hbm.at[0], fields.at[0, pl.ds(top, rows), pl.ds(PAD, cols)], local_sem.at[0]
    )
    src_copy = pltpu.make_async_copy(src_hbm.at[0], src_ref, local_sem.at[1])
    owner_copy = pltpu.make_async_copy(owner_hbm, owner_ref, local_sem.at[2])
    cond_copy.start()
    src_copy.start()
    owner_copy.start()

    for s in range(4):
        fields[s, :, 0:PAD] = jnp.zeros((rows + 16, PAD), jnp.float32)
        fields[s, :, PAD + cols :] = jnp.zeros((rows + 16, PAD), jnp.float32)
    for d, axis_end in enumerate((layer == 0, layer == n_layer - 1)):

        @pl.when(axis_end)
        def _():
            for s in range(4):
                layer_halo[s, d] = jnp.zeros((rows, cols), jnp.float32)

    for d, axis_end in enumerate((slab == 0, slab == n_slab - 1)):

        @pl.when(axis_end)
        def _():
            for s in range(4):
                for j in range(CHUNKS):
                    row_recv[s, d, j] = jnp.zeros((1, width), jnp.float32)

    sends_to = (layer < n_layer - 1, layer > 0, slab < n_slab - 1, slab > 0)
    gets_from = (layer > 0, layer < n_layer - 1, slab > 0, slab < n_slab - 1)
    target = (
        {"layer": lax.rem(layer + 1, n_layer)},
        {"layer": lax.rem(layer + n_layer - 1, n_layer)},
        {"slab": lax.rem(slab + 1, n_slab)},
        {"slab": lax.rem(slab + n_slab - 1, n_slab)},
    )

    def used(stage, direction, j):
        if stage < 3:
            return True
        return direction < 3

    def wanted(stage, direction, j, sender_layer):
        if stage == 3 and direction == 0 and j >= CHUNKS // 2:
            return sender_layer % 2 == 0
        if stage == 3 and direction == 1 and j < CHUNKS // 2:
            return sender_layer % 2 == 1
        return True

    def halo_copy(stage, direction, j):
        span = pl.ds(j * width, width)
        if direction < 2:
            source = fields.at[stage, pl.ds(top, rows), pl.ds(PAD + j * width, width)]
            dest = layer_halo.at[stage, direction, :, span]
        else:
            source = row_send.at[stage, direction - 2, j]
            dest = row_recv.at[stage, direction - 2, j]
        return pltpu.make_async_remote_copy(
            src_ref=source,
            dst_ref=dest,
            send_sem=halo_ssem.at[stage, direction, j],
            recv_sem=halo_rsem.at[stage, direction, j],
            device_id=target[direction],
            device_id_type=MESH,
        )

    def put_field(stage, j, value):
        fields[stage, top:bottom, PAD + j * width : PAD + (j + 1) * width] = value
        row_send[stage, 0, j] = value[rows - 1 : rows]
        row_send[stage, 1, j] = value[0:1]

    def send_field(stage, j):
        for direction in range(4):
            if used(stage, direction, j):

                @pl.when(sends_to[direction] & wanted(stage, direction, j, layer))
                def _():
                    halo_copy(stage, direction, j).start()

    def get_halo(stage, j):
        for direction in range(4):
            if used(stage, direction, j):

                @pl.when(gets_from[direction] & wanted(stage, direction, j, layer + 1))
                def _():
                    halo_copy(stage, direction, j).wait_recv()

        span = slice(PAD + j * width, PAD + (j + 1) * width)
        fields[stage, top - 1 : top, span] = row_recv[stage, 0, j]
        if stage < 3:
            fields[stage, bottom : bottom + 1, span] = row_recv[stage, 1, j]

    def near(stage, j, which):
        c0 = j * width
        if which == "west":
            ext = fields[stage, top:bottom, c0 : c0 + width + 2 * PAD]
            return pltpu.roll(ext, 1, 1)[:, PAD : PAD + width]
        if which == "east":
            ext = fields[stage, top:bottom, c0 : c0 + width + 2 * PAD]
            return pltpu.roll(ext, width + 2 * PAD - 1, 1)[:, PAD : PAD + width]
        span = slice(PAD + c0, PAD + c0 + width)
        if which == "north":
            return fields[stage, top - 1 : bottom - 1, span]
        if which == "south":
            return fields[stage, top + 1 : bottom + 1, span]
        return layer_halo[stage, 0 if which == "below" else 1, :, c0 : c0 + width]

    names = ("west", "east", "north", "south", "below", "above")

    def here(stage, j):
        return fields[stage, top:bottom, PAD + j * width : PAD + (j + 1) * width]

    cond_copy.wait()
    for j in range(CHUNKS):
        row_send[0, 0, j] = fields[0, bottom - 1 : bottom, PAD + j * width : PAD + (j + 1) * width]
        row_send[0, 1, j] = fields[0, top : top + 1, PAD + j * width : PAD + (j + 1) * width]
    pl.semaphore_wait(barrier, n_greet)
    for j in range(CHUNKS):
        send_field(0, j)

    owner_copy.wait()
    my_row = slab // per_tile

    def list_tiles(owner, carry):
        packed = jnp.int32(0)
        for t in range(tiles_across):
            packed = jnp.where(owner_ref[my_row, t] == owner, packed * 256 + t, packed)
        table[owner] = packed
        return carry

    lax.fori_loop(0, n_slab, list_tiles, 0)

    src_copy.wait()
    moments = [jnp.zeros((8, 128), jnp.float32) for _ in range(6)]
    for j in range(CHUNKS):
        get_halo(0, j)
        span = slice(j * width, (j + 1) * width)
        cond = here(0, j)
        diagonal = None
        for i, name in enumerate(names):
            face = cond + near(0, j, name)
            coefs[i, :, span] = face
            diagonal = face if diagonal is None else diagonal + face
        inverse = 1.0 / diagonal
        inv_ref[:, span] = inverse
        source = src_ref[:, span]
        field = source * inverse
        put_field(1, j, field)
        send_field(1, j)
        moments[0] = moments[0] + fold(field * source)
    for stage in (1, 2):
        for j in range(CHUNKS):
            get_halo(stage, j)
            span = slice(j * width, (j + 1) * width)
            image = None
            for i, name in enumerate(names):
                term = coefs[i, :, span] * near(stage, j, name)
                image = term if image is None else image + term
            field = inv_ref[:, span] * image
            put_field(stage + 1, j, field)
            send_field(stage + 1, j)
            moments[2 * stage - 1] = moments[2 * stage - 1] + fold(here(stage, j) * image)
            moments[2 * stage] = moments[2 * stage] + fold(field * image)
    for j in range(CHUNKS):
        get_halo(3, j)
        span = slice(j * width, (j + 1) * width)
        side = "below" if j < CHUNKS // 2 else "above"
        image = None
        for name in ("west", "north", side):
            term = coefs[names.index(name), :, span] * near(3, j, name)
            image = term if image is None else image + term
        moments[5] = moments[5] + fold(here(3, j) * image)
    moments[5] = 2.0 * moments[5]

    def layer_sum_copy(d):
        return pltpu.make_async_remote_copy(
            src_ref=red_layer.at[layer],
            dst_ref=red_layer.at[layer],
            send_sem=red_ssem.at[0, d],
            recv_sem=red_rsem.at[0, d],
            device_id=layer_peer(d),
            device_id_type=MESH,
        )

    def slab_sum_copy(d):
        return pltpu.make_async_remote_copy(
            src_ref=red_slab.at[slab],
            dst_ref=red_slab.at[slab],
            send_sem=red_ssem.at[1, d],
            recv_sem=red_rsem.at[1, d],
            device_id=slab_peer(d),
            device_id_type=MESH,
        )

    def tile_copy(n):
        to_pair, to_slab, device = tile_peer(n)
        return pltpu.make_async_remote_copy(
            src_ref=tile_send.at[to_pair, to_slab],
            dst_ref=tile_recv.at[pair, slab],
            send_sem=tile_ssem.at[n],
            recv_sem=tile_rsem.at[n],
            device_id=device,
            device_id_type=MESH,
        )

    sums = [jnp.sum(m, axis=0, keepdims=True) for m in moments]
    red_layer[layer] = jnp.concatenate(sums + [jnp.zeros((2, 128), jnp.float32)], axis=0)
    repeat(1, n_layer, lambda d: layer_sum_copy(d).start())
    repeat(1, n_layer, lambda d: layer_sum_copy(d).wait_recv())
    red_slab[slab] = sum(red_layer[i] for i in range(n_layer))
    repeat(1, n_slab, lambda d: slab_sum_copy(d).start())
    repeat(1, n_slab, lambda d: slab_sum_copy(d).wait_recv())
    total = jnp.sum(sum(red_slab[i] for i in range(n_slab)), axis=1, keepdims=True)
    scales = [2.0 * c for c in cg_coefficients([total[k : k + 1] for k in range(6)])]

    for j in range(CHUNKS):
        value = None
        for k in range(ITERS):
            near_field = layer_halo[k + 1, 1 - core, :, j * width : (j + 1) * width]
            term = scales[k] * (here(k + 1, j) + near_field)
            value = term if value is None else value + term
        for t in range(width // TILE):
            x_tiles[j * (width // TILE) + t] = value[:, t * TILE : (t + 1) * TILE]

    lane = lax.broadcasted_iota(jnp.int32, (rows, TILE), 1) // strip

    def pack(owner, carry):
        packed = table[owner]
        pieces = [None] * n_pair
        for q in range(capacity):
            t = lax.shift_right_logical(packed, 8 * (capacity - 1 - q)) & 255
            tile = x_tiles[t]
            tile = jnp.where(core == 1, pltpu.roll(tile, TILE - strip, 1), tile)
            for p in range(n_pair):
                shift = ((q - 2 * p) * strip) % TILE
                moved = tile if shift == 0 else pltpu.roll(tile, shift, 1)
                pieces[p] = moved if q == 0 else jnp.where(lane == q, moved, pieces[p])
        for p in range(n_pair):
            tile_send[p, owner] = pieces[p]
        return carry

    lax.fori_loop(0, n_slab, pack, 0)
    repeat(1, n_pair * n_slab, lambda n: tile_copy(n).start())

    for j in range(CHUNKS):
        value = scales[0] * here(1, j) + scales[1] * here(2, j) + scales[2] * here(3, j)
        x_buf[:, j * width : (j + 1) * width] = value
    x_copy = pltpu.make_async_copy(x_buf, x_out.at[0], local_sem.at[0])
    x_copy.start()

    tile_recv[pair, slab] = tile_send[pair, slab]
    repeat(1, n_pair * n_slab, lambda n: tile_copy(n).wait_recv())
    for i in range(n_slab):
        tile_recv[0, i] = sum(tile_recv[p, i] for p in range(n_pair))
    if tile_rows == 1:
        turned = jnp.transpose(tile_recv[0].reshape(TILE, TILE))
        for k in range(owned_count):
            g_out[k] = turned[k * strip : (k + 1) * strip]
    else:
        count = jnp.int32(0)
        picked = [jnp.int32(0)] * owned_count
        for r in range(tile_rows):
            for t in range(tiles_across):
                mine = owner_ref[r, t] == slab
                picked = [jnp.where(mine & (count == k), r, p) for k, p in enumerate(picked)]
                count = jnp.where(mine, count + 1, count)
        for k in range(owned_count):
            block = tile_recv[0, pl.ds(picked[k] * per_tile, per_tile)].reshape(TILE, TILE)
            g_out[k] = jnp.transpose(block)[0:strip]

    for stage in range(4):
        for j in range(CHUNKS):
            for direction in range(4):
                if used(stage, direction, j):

                    @pl.when(sends_to[direction] & wanted(stage, direction, j, layer))
                    def _():
                        halo_copy(stage, direction, j).wait_send()

    repeat(1, n_layer, lambda d: layer_sum_copy(d).wait_send())
    repeat(1, n_slab, lambda d: slab_sum_copy(d).wait_send())
    repeat(1, n_pair * n_slab, lambda n: tile_copy(n).wait_send())
    x_copy.wait()


def per_device(adjoint_source, conductivity, tile_owner):
    n_slab, n_layer = lax.axis_size("slab"), lax.axis_size("layer")
    depth, rows, cols = adjoint_source.shape
    owned = tile_owner.shape[0] * tile_owner.shape[1] // n_slab
    strip = TILE // n_layer
    width = cols // CHUNKS
    vmem = pl.BlockSpec(memory_space=pltpu.VMEM)
    f32 = jnp.float32
    return pl.pallas_call(
        functools.partial(kernel, n_slab, n_layer),
        out_shape=(
            jax.ShapeDtypeStruct((depth, rows, cols), f32),
            jax.ShapeDtypeStruct((owned, strip, TILE), f32),
        ),
        in_specs=[pl.BlockSpec(memory_space=pl.ANY)] * 3,
        out_specs=(pl.BlockSpec(memory_space=pl.ANY), vmem),
        scratch_shapes=[
            pltpu.VMEM((rows, cols), f32),
            pltpu.SMEM(tile_owner.shape, jnp.int32),
            pltpu.VMEM((4, rows + 16, cols + 2 * PAD), f32),
            pltpu.VMEM((6, rows, cols), f32),
            pltpu.VMEM((rows, cols), f32),
            pltpu.VMEM((4, 2, rows, cols), f32),
            pltpu.VMEM((4, 2, CHUNKS, 1, width), f32),
            pltpu.VMEM((4, 2, CHUNKS, 1, width), f32),
            pltpu.VMEM((n_layer, 8, 128), f32),
            pltpu.VMEM((n_slab, 8, 128), f32),
            pltpu.VMEM((rows, cols), f32),
            pltpu.VMEM((cols // TILE, rows, TILE), f32),
            pltpu.VMEM((n_layer // 2, n_slab, rows, TILE), f32),
            pltpu.VMEM((n_layer // 2, n_slab, rows, TILE), f32),
            pltpu.SMEM((n_slab,), jnp.int32),
            pltpu.SemaphoreType.DMA((4, 4, CHUNKS)),
            pltpu.SemaphoreType.DMA((4, 4, CHUNKS)),
            pltpu.SemaphoreType.DMA((2, max(n_slab, n_layer))),
            pltpu.SemaphoreType.DMA((2, max(n_slab, n_layer))),
            pltpu.SemaphoreType.DMA((n_layer // 2 * n_slab,)),
            pltpu.SemaphoreType.DMA((n_layer // 2 * n_slab,)),
            pltpu.SemaphoreType.DMA((3,)),
        ],
        compiler_params=pltpu.CompilerParams(
            collective_id=0, has_side_effects=True, vmem_limit_bytes=48 * 1024 * 1024
        ),
        name="stack_cg",
    )(adjoint_source, conductivity, tile_owner)


def solution(mesh):
    placed = (P("layer", "slab", None), P("layer", "slab", None), P())
    return jax.shard_map(
        per_device,
        mesh=mesh,
        in_specs=placed,
        out_specs=(P("layer", "slab", None), P("slab", "layer", None)),
        check_vma=False,
    )
```

```python
import functools

import jax
import jax.numpy as jnp
from jax import lax
from jax.experimental import pallas as pl
from jax.experimental.pallas import tpu as pltpu
from jax.sharding import PartitionSpec as P

TILE = 128
ITERS = 3
CHUNKS = 2
PAD = 128
MESH = pl.DeviceIdType.MESH


def fold(value):
    rows = sum(value[i : i + 8] for i in range(0, value.shape[0], 8))
    return sum(rows[:, i : i + 128] for i in range(0, value.shape[1], 128))


def cg_coefficients(mu):
    def inner(a, b):
        total = None
        for k in range(len(a) + len(b) - 1):
            coef = None
            for i in range(len(a)):
                if 0 <= k - i < len(b):
                    term = a[i] * b[k - i]
                    coef = term if coef is None else coef + term
            total = coef * mu[k] if total is None else total + coef * mu[k]
        return total

    def axpy(a, s, b):
        out = []
        for i in range(max(len(a), len(b))):
            if i >= len(b):
                out.append(a[i])
            elif i >= len(a):
                out.append(s * b[i])
            else:
                out.append(a[i] + s * b[i])
        return out

    one = jnp.ones_like(mu[0])
    zero = jnp.zeros_like(mu[0])
    sol, res, direction, now = [zero], [one], [one], mu[0]
    for iteration in range(ITERS):
        image = axpy(direction + [zero], -one, [zero] + direction)
        step = now / inner(direction, image)
        sol = axpy(sol, step, direction)
        if iteration + 1 < ITERS:
            res = axpy(res, -step, image)
            new = inner(res, res)
            direction = axpy(res, new / now, direction)
            now = new
    return sol


def kernel(
    n_slab,
    n_layer,
    src_hbm,
    cond_hbm,
    owner_hbm,
    x_out,
    g_out,
    src_ref,
    owner_ref,
    fields,
    coefs,
    inv_ref,
    layer_halo,
    row_send,
    row_recv,
    red_layer,
    red_slab,
    x_buf,
    x_tiles,
    tile_send,
    tile_recv,
    table,
    halo_ssem,
    halo_rsem,
    red_ssem,
    red_rsem,
    tile_ssem,
    tile_rsem,
    local_sem,
):
    slab = lax.axis_index("slab")
    layer = lax.axis_index("layer")
    rows, cols = src_ref.shape
    width = cols // CHUNKS
    top, bottom = 8, 8 + rows
    tile_rows, tiles_across = owner_ref.shape
    strip = TILE // n_layer
    capacity = max(1, tiles_across // n_slab)
    owned_count = g_out.shape[0]
    per_tile = TILE // rows

    pair, core = layer // 2, layer % 2
    n_pair = n_layer // 2

    def turn(me, d, count):
        return lax.rem(me + d, count)

    def layer_peer(d):
        return {"layer": turn(layer, d, n_layer)}

    def slab_peer(d):
        return {"slab": turn(slab, d, n_slab)}

    def tile_peer(n):
        to_pair, to_slab = turn(pair, n // n_slab, n_pair), turn(slab, n % n_slab, n_slab)
        return to_pair, to_slab, {"layer": 2 * to_pair + core, "slab": to_slab}

    def repeat(start, stop, body):
        if stop - start <= 32:
            for n in range(start, stop):
                body(n)
        else:
            lax.fori_loop(start, stop, lambda n, carry: (body(n), carry)[1], 0)

    barrier = pltpu.get_barrier_semaphore()

    def greet(device):
        pl.semaphore_signal(barrier, inc=1, device_id=device, device_id_type=MESH)

    n_greet = 0
    for d in range(1, n_layer):
        if d % 2 == 1:
            greet(layer_peer(d))
            n_greet += 1
    repeat(1, n_pair * n_slab, lambda n: greet(tile_peer(n)[2]))
    n_greet += n_pair * n_slab - 1

    cond_copy = pltpu.make_async_copy(
        cond_hbm.at[0], fields.at[0, pl.ds(top, rows), pl.ds(PAD, cols)], local_sem.at[0]
    )
    src_copy = pltpu.make_async_copy(src_hbm.at[0], src_ref, local_sem.at[1])
    owner_copy = pltpu.make_async_copy(owner_hbm, owner_ref, local_sem.at[2])
    cond_copy.start()
    src_copy.start()
    owner_copy.start()

    for s in range(4):
        fields[s, :, 0:PAD] = jnp.zeros((rows + 16, PAD), jnp.float32)
        fields[s, :, PAD + cols :] = jnp.zeros((rows + 16, PAD), jnp.float32)
    for d, axis_end in enumerate((layer == 0, layer == n_layer - 1)):

        @pl.when(axis_end)
        def _():
            for s in range(4):
                layer_halo[s, d] = jnp.zeros((rows, cols), jnp.float32)

    for d, axis_end in enumerate((slab == 0, slab == n_slab - 1)):

        @pl.when(axis_end)
        def _():
            for s in range(4):
                for j in range(CHUNKS):
                    row_recv[s, d, j] = jnp.zeros((1, width), jnp.float32)

    sends_to = (layer < n_layer - 1, layer > 0, slab < n_slab - 1, slab > 0)
    gets_from = (layer > 0, layer < n_layer - 1, slab > 0, slab < n_slab - 1)
    target = (
        {"layer": lax.rem(layer + 1, n_layer)},
        {"layer": lax.rem(layer + n_layer - 1, n_layer)},
        {"slab": lax.rem(slab + 1, n_slab)},
        {"slab": lax.rem(slab + n_slab - 1, n_slab)},
    )

    def used(stage, direction, j):
        if stage < 3:
            return True
        return direction < 3

    def wanted(stage, direction, j, sender_layer):
        if stage == 3 and direction == 0 and j >= CHUNKS // 2:
            return sender_layer % 2 == 0
        if stage == 3 and direction == 1 and j < CHUNKS // 2:
            return sender_layer % 2 == 1
        return True

    def halo_copy(stage, direction, j):
        span = pl.ds(j * width, width)
        if direction < 2:
            source = fields.at[stage, pl.ds(top, rows), pl.ds(PAD + j * width, width)]
            dest = layer_halo.at[stage, direction, :, span]
        else:
            source = row_send.at[stage, direction - 2, j]
            dest = row_recv.at[stage, direction - 2, j]
        return pltpu.make_async_remote_copy(
            src_ref=source,
            dst_ref=dest,
            send_sem=halo_ssem.at[stage, direction, j],
            recv_sem=halo_rsem.at[stage, direction, j],
            device_id=target[direction],
            device_id_type=MESH,
        )

    def put_field(stage, j, value):
        fields[stage, top:bottom, PAD + j * width : PAD + (j + 1) * width] = value
        row_send[stage, 0, j] = value[rows - 1 : rows]
        row_send[stage, 1, j] = value[0:1]

    def send_field(stage, j):
        for direction in range(4):
            if used(stage, direction, j):

                @pl.when(sends_to[direction] & wanted(stage, direction, j, layer))
                def _():
                    halo_copy(stage, direction, j).start()

    def get_halo(stage, j):
        for direction in range(4):
            if used(stage, direction, j):

                @pl.when(gets_from[direction] & wanted(stage, direction, j, layer + 1))
                def _():
                    halo_copy(stage, direction, j).wait_recv()

        span = slice(PAD + j * width, PAD + (j + 1) * width)
        fields[stage, top - 1 : top, span] = row_recv[stage, 0, j]
        if stage < 3:
            fields[stage, bottom : bottom + 1, span] = row_recv[stage, 1, j]

    def near(stage, j, which):
        c0 = j * width
        if which == "west":
            ext = fields[stage, top:bottom, c0 : c0 + width + 2 * PAD]
            return pltpu.roll(ext, 1, 1)[:, PAD : PAD + width]
        if which == "east":
            ext = fields[stage, top:bottom, c0 : c0 + width + 2 * PAD]
            return pltpu.roll(ext, width + 2 * PAD - 1, 1)[:, PAD : PAD + width]
        span = slice(PAD + c0, PAD + c0 + width)
        if which == "north":
            return fields[stage, top - 1 : bottom - 1, span]
        if which == "south":
            return fields[stage, top + 1 : bottom + 1, span]
        return layer_halo[stage, 0 if which == "below" else 1, :, c0 : c0 + width]

    names = ("west", "east", "north", "south", "below", "above")

    def here(stage, j):
        return fields[stage, top:bottom, PAD + j * width : PAD + (j + 1) * width]

    cond_copy.wait()
    for j in range(CHUNKS):
        row_send[0, 0, j] = fields[0, bottom - 1 : bottom, PAD + j * width : PAD + (j + 1) * width]
        row_send[0, 1, j] = fields[0, top : top + 1, PAD + j * width : PAD + (j + 1) * width]
    pl.semaphore_wait(barrier, n_greet)
    for j in range(CHUNKS):
        send_field(0, j)

    owner_copy.wait()
    my_row = slab // per_tile

    def list_tiles(owner, carry):
        packed = jnp.int32(0)
        for t in range(tiles_across):
            packed = jnp.where(owner_ref[my_row, t] == owner, packed * 256 + t, packed)
        table[owner] = packed
        return carry

    lax.fori_loop(0, n_slab, list_tiles, 0)

    src_copy.wait()
    moments = [jnp.zeros((8, 128), jnp.float32) for _ in range(6)]
    for j in range(CHUNKS):
        get_halo(0, j)
        span = slice(j * width, (j + 1) * width)
        cond = here(0, j)
        diagonal = None
        for i, name in enumerate(names):
            face = cond + near(0, j, name)
            coefs[i, :, span] = face
            diagonal = face if diagonal is None else diagonal + face
        inverse = 1.0 / diagonal
        inv_ref[:, span] = inverse
        source = src_ref[:, span]
        field = source * inverse
        put_field(1, j, field)
        send_field(1, j)
        moments[0] = moments[0] + fold(field * source)
    for stage in (1, 2):
        for j in range(CHUNKS):
            get_halo(stage, j)
            span = slice(j * width, (j + 1) * width)
            image = None
            for i, name in enumerate(names):
                term = coefs[i, :, span] * near(stage, j, name)
                image = term if image is None else image + term
            field = inv_ref[:, span] * image
            put_field(stage + 1, j, field)
            send_field(stage + 1, j)
            moments[2 * stage - 1] = moments[2 * stage - 1] + fold(here(stage, j) * image)
            moments[2 * stage] = moments[2 * stage] + fold(field * image)
    for j in range(CHUNKS):
        get_halo(3, j)
        span = slice(j * width, (j + 1) * width)
        side = "below" if j < CHUNKS // 2 else "above"
        image = None
        for name in ("west", "north", side):
            term = coefs[names.index(name), :, span] * near(3, j, name)
            image = term if image is None else image + term
        moments[5] = moments[5] + fold(here(3, j) * image)
    moments[5] = 2.0 * moments[5]

    def layer_sum_copy(d):
        return pltpu.make_async_remote_copy(
            src_ref=red_layer.at[layer],
            dst_ref=red_layer.at[layer],
            send_sem=red_ssem.at[0, d],
            recv_sem=red_rsem.at[0, d],
            device_id=layer_peer(d),
            device_id_type=MESH,
        )

    def slab_sum_copy(d):
        return pltpu.make_async_remote_copy(
            src_ref=red_slab.at[slab],
            dst_ref=red_slab.at[slab],
            send_sem=red_ssem.at[1, d],
            recv_sem=red_rsem.at[1, d],
            device_id=slab_peer(d),
            device_id_type=MESH,
        )

    def tile_copy(n):
        to_pair, to_slab, device = tile_peer(n)
        return pltpu.make_async_remote_copy(
            src_ref=tile_send.at[to_pair, to_slab],
            dst_ref=tile_recv.at[pair, slab],
            send_sem=tile_ssem.at[n],
            recv_sem=tile_rsem.at[n],
            device_id=device,
            device_id_type=MESH,
        )

    sums = [jnp.sum(m, axis=0, keepdims=True) for m in moments]
    red_layer[layer] = jnp.concatenate(sums + [jnp.zeros((2, 128), jnp.float32)], axis=0)
    repeat(1, n_layer, lambda d: layer_sum_copy(d).start())
    repeat(1, n_layer, lambda d: layer_sum_copy(d).wait_recv())
    red_slab[slab] = sum(red_layer[i] for i in range(n_layer))
    repeat(1, n_slab, lambda d: slab_sum_copy(d).start())
    repeat(1, n_slab, lambda d: slab_sum_copy(d).wait_recv())
    total = jnp.sum(sum(red_slab[i] for i in range(n_slab)), axis=1, keepdims=True)
    scales = [2.0 * c for c in cg_coefficients([total[k : k + 1] for k in range(6)])]

    for j in range(CHUNKS):
        value = None
        for k in range(ITERS):
            near_field = layer_halo[k + 1, 1 - core, :, j * width : (j + 1) * width]
            term = scales[k] * (here(k + 1, j) + near_field)
            value = term if value is None else value + term
        for t in range(width // TILE):
            x_tiles[j * (width // TILE) + t] = value[:, t * TILE : (t + 1) * TILE]

    lane = lax.broadcasted_iota(jnp.int32, (rows, TILE), 1) // strip

    def pack(owner, carry):
        packed = table[owner]
        pieces = [None] * n_pair
        for q in range(capacity):
            t = lax.shift_right_logical(packed, 8 * (capacity - 1 - q)) & 255
            tile = x_tiles[t]
            tile = jnp.where(core == 1, pltpu.roll(tile, TILE - strip, 1), tile)
            for p in range(n_pair):
                shift = ((q - 2 * p) * strip) % TILE
                moved = tile if shift == 0 else pltpu.roll(tile, shift, 1)
                pieces[p] = moved if q == 0 else jnp.where(lane == q, moved, pieces[p])
        for p in range(n_pair):
            tile_send[p, owner] = pieces[p]
        return carry

    lax.fori_loop(0, n_slab, pack, 0)
    repeat(1, n_pair * n_slab, lambda n: tile_copy(n).start())

    for j in range(CHUNKS):
        value = scales[0] * here(1, j) + scales[1] * here(2, j) + scales[2] * here(3, j)
        x_buf[:, j * width : (j + 1) * width] = value
    x_copy = pltpu.make_async_copy(x_buf, x_out.at[0], local_sem.at[0])
    x_copy.start()

    tile_recv[pair, slab] = tile_send[pair, slab]
    repeat(1, n_pair * n_slab, lambda n: tile_copy(n).wait_recv())
    for i in range(n_slab):
        tile_recv[0, i] = sum(tile_recv[p, i] for p in range(n_pair))
    if tile_rows == 1:
        turned = jnp.transpose(tile_recv[0].reshape(TILE, TILE))
        for k in range(owned_count):
            g_out[k] = turned[k * strip : (k + 1) * strip]
    else:
        count = jnp.int32(0)
        picked = [jnp.int32(0)] * owned_count
        for r in range(tile_rows):
            for t in range(tiles_across):
                mine = owner_ref[r, t] == slab
                picked = [jnp.where(mine & (count == k), r, p) for k, p in enumerate(picked)]
                count = jnp.where(mine, count + 1, count)
        for k in range(owned_count):
            block = tile_recv[0, pl.ds(picked[k] * per_tile, per_tile)].reshape(TILE, TILE)
            g_out[k] = jnp.transpose(block)[0:strip]

    for stage in range(4):
        for j in range(CHUNKS):
            for direction in range(4):
                if used(stage, direction, j):

                    @pl.when(sends_to[direction] & wanted(stage, direction, j, layer))
                    def _():
                        halo_copy(stage, direction, j).wait_send()

    repeat(1, n_layer, lambda d: layer_sum_copy(d).wait_send())
    repeat(1, n_slab, lambda d: slab_sum_copy(d).wait_send())
    repeat(1, n_pair * n_slab, lambda n: tile_copy(n).wait_send())
    x_copy.wait()


def per_device(adjoint_source, conductivity, tile_owner):
    n_slab, n_layer = lax.axis_size("slab"), lax.axis_size("layer")
    depth, rows, cols = adjoint_source.shape
    owned = tile_owner.shape[0] * tile_owner.shape[1] // n_slab
    strip = TILE // n_layer
    width = cols // CHUNKS
    vmem = pl.BlockSpec(memory_space=pltpu.VMEM)
    f32 = jnp.float32
    return pl.pallas_call(
        functools.partial(kernel, n_slab, n_layer),
        out_shape=(
            jax.ShapeDtypeStruct((depth, rows, cols), f32),
            jax.ShapeDtypeStruct((owned, strip, TILE), f32),
        ),
        in_specs=[pl.BlockSpec(memory_space=pltpu.HBM)] * 3,
        out_specs=(pl.BlockSpec(memory_space=pl.ANY), vmem),
        scratch_shapes=[
            pltpu.VMEM((rows, cols), f32),
            pltpu.SMEM(tile_owner.shape, jnp.int32),
            pltpu.VMEM((4, rows + 16, cols + 2 * PAD), f32),
            pltpu.VMEM((6, rows, cols), f32),
            pltpu.VMEM((rows, cols), f32),
            pltpu.VMEM((4, 2, rows, cols), f32),
            pltpu.VMEM((4, 2, CHUNKS, 1, width), f32),
            pltpu.VMEM((4, 2, CHUNKS, 1, width), f32),
            pltpu.VMEM((n_layer, 8, 128), f32),
            pltpu.VMEM((n_slab, 8, 128), f32),
            pltpu.VMEM((rows, cols), f32),
            pltpu.VMEM((cols // TILE, rows, TILE), f32),
            pltpu.VMEM((n_layer // 2, n_slab, rows, TILE), f32),
            pltpu.VMEM((n_layer // 2, n_slab, rows, TILE), f32),
            pltpu.SMEM((n_slab,), jnp.int32),
            pltpu.SemaphoreType.DMA((4, 4, CHUNKS)),
            pltpu.SemaphoreType.DMA((4, 4, CHUNKS)),
            pltpu.SemaphoreType.DMA((2, max(n_slab, n_layer))),
            pltpu.SemaphoreType.DMA((2, max(n_slab, n_layer))),
            pltpu.SemaphoreType.DMA((n_layer // 2 * n_slab,)),
            pltpu.SemaphoreType.DMA((n_layer // 2 * n_slab,)),
            pltpu.SemaphoreType.DMA((3,)),
        ],
        compiler_params=pltpu.CompilerParams(
            collective_id=0, has_side_effects=True, vmem_limit_bytes=48 * 1024 * 1024
        ),
        name="stack_cg",
    )(adjoint_source, conductivity, tile_owner)


def solution(mesh):
    placed = (P("layer", "slab", None), P("layer", "slab", None), P())
    return jax.shard_map(
        per_device,
        mesh=mesh,
        in_specs=placed,
        out_specs=(P("layer", "slab", None), P("slab", "layer", None)),
        check_vma=False,
    )
```

```python
import functools

import jax
import jax.numpy as jnp
from jax import lax
from jax.experimental import pallas as pl
from jax.experimental.pallas import tpu as pltpu
from jax.sharding import PartitionSpec as P

TILE = 128
ITERS = 3
CHUNKS = 4
PAD = 128
MESH = pl.DeviceIdType.MESH


def fold(value):
    rows = sum(value[i : i + 8] for i in range(0, value.shape[0], 8))
    return sum(rows[:, i : i + 128] for i in range(0, value.shape[1], 128))


def cg_coefficients(mu):
    def inner(a, b):
        total = None
        for k in range(len(a) + len(b) - 1):
            coef = None
            for i in range(len(a)):
                if 0 <= k - i < len(b):
                    term = a[i] * b[k - i]
                    coef = term if coef is None else coef + term
            total = coef * mu[k] if total is None else total + coef * mu[k]
        return total

    def axpy(a, s, b):
        out = []
        for i in range(max(len(a), len(b))):
            if i >= len(b):
                out.append(a[i])
            elif i >= len(a):
                out.append(s * b[i])
            else:
                out.append(a[i] + s * b[i])
        return out

    one = jnp.ones_like(mu[0])
    zero = jnp.zeros_like(mu[0])
    sol, res, direction, now = [zero], [one], [one], mu[0]
    for iteration in range(ITERS):
        image = axpy(direction + [zero], -one, [zero] + direction)
        step = now / inner(direction, image)
        sol = axpy(sol, step, direction)
        if iteration + 1 < ITERS:
            res = axpy(res, -step, image)
            new = inner(res, res)
            direction = axpy(res, new / now, direction)
            now = new
    return sol


def kernel(
    n_slab,
    n_layer,
    src_hbm,
    cond_hbm,
    owner_hbm,
    x_out,
    g_out,
    src_ref,
    owner_ref,
    fields,
    coefs,
    inv_ref,
    layer_halo,
    row_send,
    row_recv,
    red_layer,
    red_slab,
    x_buf,
    x_tiles,
    tile_send,
    tile_recv,
    tiles,
    g_buf,
    table,
    halo_ssem,
    halo_rsem,
    red_ssem,
    red_rsem,
    tile_ssem,
    tile_rsem,
    local_sem,
):
    slab = lax.axis_index("slab")
    layer = lax.axis_index("layer")
    rows, cols = src_ref.shape
    width = cols // CHUNKS
    top, bottom = 8, 8 + rows
    tile_rows, tiles_across = owner_ref.shape
    strip = TILE // n_layer
    capacity = max(1, tiles_across // n_slab)
    owned_count = g_out.shape[0]
    per_tile = TILE // rows

    pair, core = layer // 2, layer % 2
    n_pair = n_layer // 2

    def turn(me, d, count):
        return lax.rem(me + d, count)

    def layer_peer(d):
        return {"layer": turn(layer, d, n_layer)}

    def slab_peer(d):
        return {"slab": turn(slab, d, n_slab)}

    def tile_peer(n):
        to_pair, to_slab = turn(pair, n // n_slab, n_pair), turn(slab, n % n_slab, n_slab)
        return to_pair, to_slab, {"layer": 2 * to_pair + core, "slab": to_slab}

    def repeat(start, stop, body):
        if stop - start <= 32:
            for n in range(start, stop):
                body(n)
        else:
            lax.fori_loop(start, stop, lambda n, carry: (body(n), carry)[1], 0)

    barrier = pltpu.get_barrier_semaphore()

    def greet(device):
        pl.semaphore_signal(barrier, inc=1, device_id=device, device_id_type=MESH)

    n_greet = 0
    for d in range(1, n_layer):
        if d % 2 == 1:
            greet(layer_peer(d))
            n_greet += 1
    repeat(1, n_pair * n_slab, lambda n: greet(tile_peer(n)[2]))
    n_greet += n_pair * n_slab - 1

    cond_copy = pltpu.make_async_copy(
        cond_hbm.at[0], fields.at[0, pl.ds(top, rows), pl.ds(PAD, cols)], local_sem.at[0]
    )
    src_copy = pltpu.make_async_copy(src_hbm.at[0], src_ref, local_sem.at[1])
    owner_copy = pltpu.make_async_copy(owner_hbm, owner_ref, local_sem.at[2])
    cond_copy.start()
    src_copy.start()
    owner_copy.start()

    for s in range(4):
        fields[s, :, 0:PAD] = jnp.zeros((rows + 16, PAD), jnp.float32)
        fields[s, :, PAD + cols :] = jnp.zeros((rows + 16, PAD), jnp.float32)
    for d, axis_end in enumerate((layer == 0, layer == n_layer - 1)):

        @pl.when(axis_end)
        def _():
            for s in range(4):
                layer_halo[s, d] = jnp.zeros((rows, cols), jnp.float32)

    for d, axis_end in enumerate((slab == 0, slab == n_slab - 1)):

        @pl.when(axis_end)
        def _():
            for s in range(4):
                for j in range(CHUNKS):
                    row_recv[s, d, j] = jnp.zeros((1, width), jnp.float32)

    sends_to = (layer < n_layer - 1, layer > 0, slab < n_slab - 1, slab > 0)
    gets_from = (layer > 0, layer < n_layer - 1, slab > 0, slab < n_slab - 1)
    target = (
        {"layer": lax.rem(layer + 1, n_layer)},
        {"layer": lax.rem(layer + n_layer - 1, n_layer)},
        {"slab": lax.rem(slab + 1, n_slab)},
        {"slab": lax.rem(slab + n_slab - 1, n_slab)},
    )

    def used(stage, direction, j):
        if stage < 3:
            return True
        return direction < 3

    def wanted(stage, direction, j, sender_layer):
        if stage == 3 and direction == 0 and j >= CHUNKS // 2:
            return sender_layer % 2 == 0
        if stage == 3 and direction == 1 and j < CHUNKS // 2:
            return sender_layer % 2 == 1
        return True

    def halo_copy(stage, direction, j):
        span = pl.ds(j * width, width)
        if direction < 2:
            source = fields.at[stage, pl.ds(top, rows), pl.ds(PAD + j * width, width)]
            dest = layer_halo.at[stage, direction, :, span]
        else:
            source = row_send.at[stage, direction - 2, j]
            dest = row_recv.at[stage, direction - 2, j]
        return pltpu.make_async_remote_copy(
            src_ref=source,
            dst_ref=dest,
            send_sem=halo_ssem.at[stage, direction, j],
            recv_sem=halo_rsem.at[stage, direction, j],
            device_id=target[direction],
            device_id_type=MESH,
        )

    def put_field(stage, j, value):
        fields[stage, top:bottom, PAD + j * width : PAD + (j + 1) * width] = value
        row_send[stage, 0, j] = value[rows - 1 : rows]
        row_send[stage, 1, j] = value[0:1]

    def send_field(stage, j):
        for direction in range(4):
            if used(stage, direction, j):

                @pl.when(sends_to[direction] & wanted(stage, direction, j, layer))
                def _():
                    halo_copy(stage, direction, j).start()

    def get_halo(stage, j):
        for direction in range(4):
            if used(stage, direction, j):

                @pl.when(gets_from[direction] & wanted(stage, direction, j, layer + 1))
                def _():
                    halo_copy(stage, direction, j).wait_recv()

        span = slice(PAD + j * width, PAD + (j + 1) * width)
        fields[stage, top - 1 : top, span] = row_recv[stage, 0, j]
        if stage < 3:
            fields[stage, bottom : bottom + 1, span] = row_recv[stage, 1, j]

    def near(stage, j, which):
        c0 = j * width
        if which == "west":
            ext = fields[stage, top:bottom, c0 : c0 + width + 2 * PAD]
            return pltpu.roll(ext, 1, 1)[:, PAD : PAD + width]
        if which == "east":
            ext = fields[stage, top:bottom, c0 : c0 + width + 2 * PAD]
            return pltpu.roll(ext, width + 2 * PAD - 1, 1)[:, PAD : PAD + width]
        span = slice(PAD + c0, PAD + c0 + width)
        if which == "north":
            return fields[stage, top - 1 : bottom - 1, span]
        if which == "south":
            return fields[stage, top + 1 : bottom + 1, span]
        return layer_halo[stage, 0 if which == "below" else 1, :, c0 : c0 + width]

    names = ("west", "east", "north", "south", "below", "above")

    def here(stage, j):
        return fields[stage, top:bottom, PAD + j * width : PAD + (j + 1) * width]

    cond_copy.wait()
    for j in range(CHUNKS):
        row_send[0, 0, j] = fields[0, bottom - 1 : bottom, PAD + j * width : PAD + (j + 1) * width]
        row_send[0, 1, j] = fields[0, top : top + 1, PAD + j * width : PAD + (j + 1) * width]
    pl.semaphore_wait(barrier, n_greet)
    for j in range(CHUNKS):
        send_field(0, j)

    owner_copy.wait()
    my_row = slab // per_tile

    def list_tiles(owner, carry):
        packed = jnp.int32(0)
        for t in range(tiles_across):
            packed = jnp.where(owner_ref[my_row, t] == owner, packed * 256 + t, packed)
        table[owner] = packed
        return carry

    lax.fori_loop(0, n_slab, list_tiles, 0)

    def layer_sum_copy(d):
        return pltpu.make_async_remote_copy(
            src_ref=red_layer.at[layer],
            dst_ref=red_layer.at[layer],
            send_sem=red_ssem.at[0, d],
            recv_sem=red_rsem.at[0, d],
            device_id=layer_peer(d),
            device_id_type=MESH,
        )

    def slab_sum_copy(d):
        return pltpu.make_async_remote_copy(
            src_ref=red_slab.at[slab],
            dst_ref=red_slab.at[slab],
            send_sem=red_ssem.at[1, d],
            recv_sem=red_rsem.at[1, d],
            device_id=slab_peer(d),
            device_id_type=MESH,
        )

    def tile_copy(k, n):
        to_pair, to_slab, device = tile_peer(n)
        return pltpu.make_async_remote_copy(
            src_ref=tile_send.at[k, to_pair, to_slab],
            dst_ref=tile_recv.at[k, pair, slab],
            send_sem=tile_ssem.at[k, n],
            recv_sem=tile_rsem.at[k, n],
            device_id=device,
            device_id_type=MESH,
        )

    lane = lax.broadcasted_iota(jnp.int32, (rows, TILE), 1) // strip

    def deliver(k):
        for j in range(CHUNKS):
            value = here(k + 1, j) + layer_halo[k + 1, 1 - core, :, j * width : (j + 1) * width]
            for t in range(width // TILE):
                x_tiles[j * (width // TILE) + t] = value[:, t * TILE : (t + 1) * TILE]

        def pack(owner, carry):
            packed = table[owner]
            pieces = [None] * n_pair
            for q in range(capacity):
                t = lax.shift_right_logical(packed, 8 * (capacity - 1 - q)) & 255
                tile = x_tiles[t]
                tile = jnp.where(core == 1, pltpu.roll(tile, TILE - strip, 1), tile)
                for p in range(n_pair):
                    shift = ((q - 2 * p) * strip) % TILE
                    moved = tile if shift == 0 else pltpu.roll(tile, shift, 1)
                    pieces[p] = moved if q == 0 else jnp.where(lane == q, moved, pieces[p])
            for p in range(n_pair):
                tile_send[k, p, owner] = pieces[p]
            return carry

        lax.fori_loop(0, n_slab, pack, 0)
        repeat(1, n_pair * n_slab, lambda n: tile_copy(k, n).start())
        tile_recv[k, pair, slab] = tile_send[k, pair, slab]

    src_copy.wait()
    moments = [jnp.zeros((8, 128), jnp.float32) for _ in range(6)]
    for j in range(CHUNKS):
        get_halo(0, j)
        span = slice(j * width, (j + 1) * width)
        cond = here(0, j)
        diagonal = None
        for i, name in enumerate(names):
            face = cond + near(0, j, name)
            coefs[i, :, span] = face
            diagonal = face if diagonal is None else diagonal + face
        inverse = 1.0 / diagonal
        inv_ref[:, span] = inverse
        source = src_ref[:, span]
        field = source * inverse
        put_field(1, j, field)
        send_field(1, j)
        moments[0] = moments[0] + fold(field * source)
    for stage in (1, 2):
        for j in range(CHUNKS):
            get_halo(stage, j)
            span = slice(j * width, (j + 1) * width)
            image = None
            for i, name in enumerate(names):
                term = coefs[i, :, span] * near(stage, j, name)
                image = term if image is None else image + term
            field = inv_ref[:, span] * image
            put_field(stage + 1, j, field)
            send_field(stage + 1, j)
            moments[2 * stage - 1] = moments[2 * stage - 1] + fold(here(stage, j) * image)
            moments[2 * stage] = moments[2 * stage] + fold(field * image)
        deliver(stage - 1)
    for j in range(CHUNKS):
        get_halo(3, j)
        span = slice(j * width, (j + 1) * width)
        side = "below" if j < CHUNKS // 2 else "above"
        image = None
        for name in ("west", "north", side):
            term = coefs[names.index(name), :, span] * near(3, j, name)
            image = term if image is None else image + term
        moments[5] = moments[5] + fold(here(3, j) * image)
    moments[5] = 2.0 * moments[5]

    sums = [jnp.sum(m, axis=0, keepdims=True) for m in moments]
    red_layer[layer] = jnp.concatenate(sums + [jnp.zeros((2, 128), jnp.float32)], axis=0)
    repeat(1, n_layer, lambda d: layer_sum_copy(d).start())
    deliver(2)
    repeat(1, n_layer, lambda d: layer_sum_copy(d).wait_recv())
    red_slab[slab] = sum(red_layer[i] for i in range(n_layer))
    repeat(1, n_slab, lambda d: slab_sum_copy(d).start())
    repeat(1, n_slab, lambda d: slab_sum_copy(d).wait_recv())
    total = jnp.sum(sum(red_slab[i] for i in range(n_slab)), axis=1, keepdims=True)
    scales = [2.0 * c for c in cg_coefficients([total[k : k + 1] for k in range(6)])]

    for j in range(CHUNKS):
        value = scales[0] * here(1, j) + scales[1] * here(2, j) + scales[2] * here(3, j)
        x_buf[:, j * width : (j + 1) * width] = value
    x_copy = pltpu.make_async_copy(x_buf, x_out.at[0], local_sem.at[0])
    x_copy.start()

    for k in range(ITERS):
        repeat(1, n_pair * n_slab, lambda n: tile_copy(k, n).wait_recv())

    def combine(i, carry):
        value = None
        for k in range(ITERS):
            term = scales[k] * sum(tile_recv[k, p, i] for p in range(n_pair))
            value = term if value is None else value + term
        tiles[i] = value
        return carry

    lax.fori_loop(0, n_slab, combine, 0)
    if tile_rows == 1:
        turned = jnp.transpose(tiles[...].reshape(TILE, TILE))
        for k in range(owned_count):
            g_buf[k] = turned[k * strip : (k + 1) * strip]
    else:
        count = jnp.int32(0)
        picked = [jnp.int32(0)] * owned_count
        for r in range(tile_rows):
            for t in range(tiles_across):
                mine = owner_ref[r, t] == slab
                picked = [jnp.where(mine & (count == k), r, p) for k, p in enumerate(picked)]
                count = jnp.where(mine, count + 1, count)
        for k in range(owned_count):
            block = tiles[pl.ds(picked[k] * per_tile, per_tile)].reshape(TILE, TILE)
            g_buf[k] = jnp.transpose(block)[0:strip]

    g_copy = pltpu.make_async_copy(g_buf, g_out, local_sem.at[1])
    g_copy.start()

    for stage in range(4):
        for j in range(CHUNKS):
            for direction in range(4):
                if used(stage, direction, j):

                    @pl.when(sends_to[direction] & wanted(stage, direction, j, layer))
                    def _():
                        halo_copy(stage, direction, j).wait_send()

    repeat(1, n_layer, lambda d: layer_sum_copy(d).wait_send())
    repeat(1, n_slab, lambda d: slab_sum_copy(d).wait_send())
    for k in range(ITERS):
        repeat(1, n_pair * n_slab, lambda n: tile_copy(k, n).wait_send())
    x_copy.wait()
    g_copy.wait()


def per_device(adjoint_source, conductivity, tile_owner):
    n_slab, n_layer = lax.axis_size("slab"), lax.axis_size("layer")
    depth, rows, cols = adjoint_source.shape
    owned = tile_owner.shape[0] * tile_owner.shape[1] // n_slab
    strip = TILE // n_layer
    width = cols // CHUNKS
    f32 = jnp.float32
    return pl.pallas_call(
        functools.partial(kernel, n_slab, n_layer),
        out_shape=(
            jax.ShapeDtypeStruct((depth, rows, cols), f32),
            jax.ShapeDtypeStruct((owned, strip, TILE), f32),
        ),
        in_specs=[pl.BlockSpec(memory_space=pltpu.HBM)] * 3,
        out_specs=(pl.BlockSpec(memory_space=pl.ANY), pl.BlockSpec(memory_space=pl.ANY)),
        scratch_shapes=[
            pltpu.VMEM((rows, cols), f32),
            pltpu.SMEM(tile_owner.shape, jnp.int32),
            pltpu.VMEM((4, rows + 16, cols + 2 * PAD), f32),
            pltpu.VMEM((6, rows, cols), f32),
            pltpu.VMEM((rows, cols), f32),
            pltpu.VMEM((4, 2, rows, cols), f32),
            pltpu.VMEM((4, 2, CHUNKS, 1, width), f32),
            pltpu.VMEM((4, 2, CHUNKS, 1, width), f32),
            pltpu.VMEM((n_layer, 8, 128), f32),
            pltpu.VMEM((n_slab, 8, 128), f32),
            pltpu.VMEM((rows, cols), f32),
            pltpu.VMEM((cols // TILE, rows, TILE), f32),
            pltpu.VMEM((ITERS, n_layer // 2, n_slab, rows, TILE), f32),
            pltpu.VMEM((ITERS, n_layer // 2, n_slab, rows, TILE), f32),
            pltpu.VMEM((n_slab, rows, TILE), f32),
            pltpu.VMEM((owned, strip, TILE), f32),
            pltpu.SMEM((n_slab,), jnp.int32),
            pltpu.SemaphoreType.DMA((4, 4, CHUNKS)),
            pltpu.SemaphoreType.DMA((4, 4, CHUNKS)),
            pltpu.SemaphoreType.DMA((2, max(n_slab, n_layer))),
            pltpu.SemaphoreType.DMA((2, max(n_slab, n_layer))),
            pltpu.SemaphoreType.DMA((ITERS, n_layer // 2 * n_slab)),
            pltpu.SemaphoreType.DMA((ITERS, n_layer // 2 * n_slab)),
            pltpu.SemaphoreType.DMA((3,)),
        ],
        compiler_params=pltpu.CompilerParams(
            collective_id=0, has_side_effects=True, vmem_limit_bytes=63 * 1024 * 1024
        ),
        name="stack_cg",
    )(adjoint_source, conductivity, tile_owner)


def solution(mesh):
    placed = (P("layer", "slab", None), P("layer", "slab", None), P())
    return jax.shard_map(
        per_device,
        mesh=mesh,
        in_specs=placed,
        out_specs=(P("layer", "slab", None), P("slab", "layer", None)),
        check_vma=False,
    )
```

```python
import functools

import jax
import jax.numpy as jnp
from jax import lax
from jax.experimental import pallas as pl
from jax.experimental.pallas import tpu as pltpu
from jax.sharding import PartitionSpec as P

TILE = 128
ITERS = 3
CHUNKS = 4
ROW_CHUNKS = 2
PAD = 128
MESH = pl.DeviceIdType.MESH


def fold(value):
    rows = sum(value[i : i + 8] for i in range(0, value.shape[0], 8))
    return sum(rows[:, i : i + 128] for i in range(0, value.shape[1], 128))


def cg_coefficients(mu):
    def inner(a, b):
        total = None
        for k in range(len(a) + len(b) - 1):
            coef = None
            for i in range(len(a)):
                if 0 <= k - i < len(b):
                    term = a[i] * b[k - i]
                    coef = term if coef is None else coef + term
            total = coef * mu[k] if total is None else total + coef * mu[k]
        return total

    def axpy(a, s, b):
        out = []
        for i in range(max(len(a), len(b))):
            if i >= len(b):
                out.append(a[i])
            elif i >= len(a):
                out.append(s * b[i])
            else:
                out.append(a[i] + s * b[i])
        return out

    one = jnp.ones_like(mu[0])
    zero = jnp.zeros_like(mu[0])
    sol, res, direction, now = [zero], [one], [one], mu[0]
    for iteration in range(ITERS):
        image = axpy(direction + [zero], -one, [zero] + direction)
        step = now / inner(direction, image)
        sol = axpy(sol, step, direction)
        if iteration + 1 < ITERS:
            res = axpy(res, -step, image)
            new = inner(res, res)
            direction = axpy(res, new / now, direction)
            now = new
    return sol


def kernel(
    n_slab,
    n_layer,
    src_hbm,
    cond_hbm,
    owner_hbm,
    x_out,
    g_out,
    src_ref,
    owner_ref,
    fields,
    coefs,
    inv_ref,
    layer_halo,
    row_send,
    row_recv,
    red_layer,
    red_slab,
    x_buf,
    x_tiles,
    tile_send,
    tile_recv,
    tiles,
    g_buf,
    table,
    halo_ssem,
    halo_rsem,
    red_ssem,
    red_rsem,
    tile_ssem,
    tile_rsem,
    local_sem,
):
    slab = lax.axis_index("slab")
    layer = lax.axis_index("layer")
    rows, cols = src_ref.shape
    width = cols // CHUNKS
    per_row = CHUNKS // ROW_CHUNKS
    top, bottom = 8, 8 + rows
    tile_rows, tiles_across = owner_ref.shape
    strip = TILE // n_layer
    capacity = max(1, tiles_across // n_slab)
    owned_count = g_out.shape[0]
    per_tile = TILE // rows

    pair, core = layer // 2, layer % 2
    n_pair = n_layer // 2

    def turn(me, d, count):
        return lax.rem(me + d, count)

    def layer_peer(d):
        return {"layer": turn(layer, d, n_layer)}

    def slab_peer(d):
        return {"slab": turn(slab, d, n_slab)}

    def tile_peer(n):
        to_pair, to_slab = turn(pair, n // n_slab, n_pair), turn(slab, n % n_slab, n_slab)
        return to_pair, to_slab, {"layer": 2 * to_pair + core, "slab": to_slab}

    def repeat(start, stop, body):
        if stop - start <= 32:
            for n in range(start, stop):
                body(n)
        else:
            lax.fori_loop(start, stop, lambda n, carry: (body(n), carry)[1], 0)

    barrier = pltpu.get_barrier_semaphore()

    def greet(device):
        pl.semaphore_signal(barrier, inc=1, device_id=device, device_id_type=MESH)

    n_greet = 0
    for d in range(1, n_layer):
        if d % 2 == 1:
            greet(layer_peer(d))
            n_greet += 1
    repeat(1, n_pair * n_slab, lambda n: greet(tile_peer(n)[2]))
    n_greet += n_pair * n_slab - 1

    cond_copy = pltpu.make_async_copy(
        cond_hbm.at[0], fields.at[0, pl.ds(top, rows), pl.ds(PAD, cols)], local_sem.at[0]
    )
    src_copy = pltpu.make_async_copy(src_hbm.at[0], src_ref, local_sem.at[1])
    owner_copy = pltpu.make_async_copy(owner_hbm, owner_ref, local_sem.at[2])
    cond_copy.start()
    src_copy.start()
    owner_copy.start()

    for s in range(4):
        fields[s, :, 0:PAD] = jnp.zeros((rows + 16, PAD), jnp.float32)
        fields[s, :, PAD + cols :] = jnp.zeros((rows + 16, PAD), jnp.float32)
    for d, axis_end in enumerate((layer == 0, layer == n_layer - 1)):

        @pl.when(axis_end)
        def _():
            for s in range(4):
                layer_halo[s, d] = jnp.zeros((rows, cols), jnp.float32)

    for d, axis_end in enumerate((slab == 0, slab == n_slab - 1)):

        @pl.when(axis_end)
        def _():
            for s in range(4):
                for j in range(ROW_CHUNKS):
                    row_recv[s, d, j] = jnp.zeros((1, cols // ROW_CHUNKS), jnp.float32)

    sends_to = (layer < n_layer - 1, layer > 0, slab < n_slab - 1, slab > 0)
    gets_from = (layer > 0, layer < n_layer - 1, slab > 0, slab < n_slab - 1)
    target = (
        {"layer": lax.rem(layer + 1, n_layer)},
        {"layer": lax.rem(layer + n_layer - 1, n_layer)},
        {"slab": lax.rem(slab + 1, n_slab)},
        {"slab": lax.rem(slab + n_slab - 1, n_slab)},
    )

    def used(stage, direction, j):
        if stage < 3:
            return True
        return direction < 3

    def wanted(stage, direction, j, sender_layer):
        if stage == 3 and direction == 0 and j >= CHUNKS // 2:
            return sender_layer % 2 == 0
        if stage == 3 and direction == 1 and j < CHUNKS // 2:
            return sender_layer % 2 == 1
        return True

    def halo_copy(stage, direction, j):
        span = pl.ds(j * width, width)
        slot = j if direction < 2 else j // per_row
        if direction < 2:
            source = fields.at[stage, pl.ds(top, rows), pl.ds(PAD + j * width, width)]
            dest = layer_halo.at[stage, direction, :, span]
        else:
            source = row_send.at[stage, direction - 2, j // per_row]
            dest = row_recv.at[stage, direction - 2, j // per_row]
        return pltpu.make_async_remote_copy(
            src_ref=source,
            dst_ref=dest,
            send_sem=halo_ssem.at[stage, direction, slot],
            recv_sem=halo_rsem.at[stage, direction, slot],
            device_id=target[direction],
            device_id_type=MESH,
        )

    def put_field(stage, j, value):
        fields[stage, top:bottom, PAD + j * width : PAD + (j + 1) * width] = value
        part = slice((j % per_row) * width, (j % per_row + 1) * width)
        row_send[stage, 0, j // per_row, :, part] = value[rows - 1 : rows]
        row_send[stage, 1, j // per_row, :, part] = value[0:1]

    def sent_with(stage, direction, j):
        return used(stage, direction, j) and (direction < 2 or j % per_row == per_row - 1)

    def got_with(stage, direction, j):
        return used(stage, direction, j) and (direction < 2 or j % per_row == 0)

    def send_field(stage, j):
        for direction in range(4):
            if sent_with(stage, direction, j):

                @pl.when(sends_to[direction] & wanted(stage, direction, j, layer))
                def _():
                    halo_copy(stage, direction, j).start()

    def get_halo(stage, j):
        for direction in range(4):
            if got_with(stage, direction, j):

                @pl.when(gets_from[direction] & wanted(stage, direction, j, layer + 1))
                def _():
                    halo_copy(stage, direction, j).wait_recv()

        span = slice(PAD + j * width, PAD + (j + 1) * width)
        part = slice((j % per_row) * width, (j % per_row + 1) * width)
        fields[stage, top - 1 : top, span] = row_recv[stage, 0, j // per_row, :, part]
        if stage < 3:
            fields[stage, bottom : bottom + 1, span] = row_recv[stage, 1, j // per_row, :, part]

    def near(stage, j, which):
        c0 = j * width
        if which == "west":
            ext = fields[stage, top:bottom, c0 : c0 + width + 2 * PAD]
            return pltpu.roll(ext, 1, 1)[:, PAD : PAD + width]
        if which == "east":
            ext = fields[stage, top:bottom, c0 : c0 + width + 2 * PAD]
            return pltpu.roll(ext, width + 2 * PAD - 1, 1)[:, PAD : PAD + width]
        span = slice(PAD + c0, PAD + c0 + width)
        if which == "north":
            return fields[stage, top - 1 : bottom - 1, span]
        if which == "south":
            return fields[stage, top + 1 : bottom + 1, span]
        return layer_halo[stage, 0 if which == "below" else 1, :, c0 : c0 + width]

    names = ("west", "east", "north", "south", "below", "above")

    def here(stage, j):
        return fields[stage, top:bottom, PAD + j * width : PAD + (j + 1) * width]

    cond_copy.wait()
    for j in range(CHUNKS):
        part = slice((j % per_row) * width, (j % per_row + 1) * width)
        span = slice(PAD + j * width, PAD + (j + 1) * width)
        row_send[0, 0, j // per_row, :, part] = fields[0, bottom - 1 : bottom, span]
        row_send[0, 1, j // per_row, :, part] = fields[0, top : top + 1, span]
    pl.semaphore_wait(barrier, n_greet)
    for j in range(CHUNKS):
        send_field(0, j)

    owner_copy.wait()
    my_row = slab // per_tile

    def list_tiles(owner, carry):
        packed = jnp.int32(0)
        for t in range(tiles_across):
            packed = jnp.where(owner_ref[my_row, t] == owner, packed * 256 + t, packed)
        table[owner] = packed
        return carry

    lax.fori_loop(0, n_slab, list_tiles, 0)

    def layer_sum_copy(d):
        return pltpu.make_async_remote_copy(
            src_ref=red_layer.at[layer],
            dst_ref=red_layer.at[layer],
            send_sem=red_ssem.at[0, d],
            recv_sem=red_rsem.at[0, d],
            device_id=layer_peer(d),
            device_id_type=MESH,
        )

    def slab_sum_copy(d):
        return pltpu.make_async_remote_copy(
            src_ref=red_slab.at[slab],
            dst_ref=red_slab.at[slab],
            send_sem=red_ssem.at[1, d],
            recv_sem=red_rsem.at[1, d],
            device_id=slab_peer(d),
            device_id_type=MESH,
        )

    def tile_copy(k, n):
        to_pair, to_slab, device = tile_peer(n)
        return pltpu.make_async_remote_copy(
            src_ref=tile_send.at[k, to_pair, to_slab],
            dst_ref=tile_recv.at[k, pair, slab],
            send_sem=tile_ssem.at[k, n],
            recv_sem=tile_rsem.at[k, n],
            device_id=device,
            device_id_type=MESH,
        )

    lane = lax.broadcasted_iota(jnp.int32, (rows, TILE), 1) // strip

    def deliver(k):
        for j in range(CHUNKS):
            value = here(k + 1, j) + layer_halo[k + 1, 1 - core, :, j * width : (j + 1) * width]
            for t in range(width // TILE):
                x_tiles[j * (width // TILE) + t] = value[:, t * TILE : (t + 1) * TILE]

        def pack(owner, carry):
            packed = table[owner]
            pieces = [None] * n_pair
            for q in range(capacity):
                t = lax.shift_right_logical(packed, 8 * (capacity - 1 - q)) & 255
                tile = x_tiles[t]
                tile = jnp.where(core == 1, pltpu.roll(tile, TILE - strip, 1), tile)
                for p in range(n_pair):
                    shift = ((q - 2 * p) * strip) % TILE
                    moved = tile if shift == 0 else pltpu.roll(tile, shift, 1)
                    pieces[p] = moved if q == 0 else jnp.where(lane == q, moved, pieces[p])
            for p in range(n_pair):
                tile_send[k, p, owner] = pieces[p]
            return carry

        lax.fori_loop(0, n_slab, pack, 0)
        repeat(1, n_pair * n_slab, lambda n: tile_copy(k, n).start())
        tile_recv[k, pair, slab] = tile_send[k, pair, slab]

    src_copy.wait()
    moments = [jnp.zeros((8, 128), jnp.float32) for _ in range(6)]
    for j in range(CHUNKS):
        get_halo(0, j)
        span = slice(j * width, (j + 1) * width)
        cond = here(0, j)
        diagonal = None
        for i, name in enumerate(names):
            face = cond + near(0, j, name)
            coefs[i, :, span] = face
            diagonal = face if diagonal is None else diagonal + face
        inverse = 1.0 / diagonal
        inv_ref[:, span] = inverse
        source = src_ref[:, span]
        field = source * inverse
        put_field(1, j, field)
        send_field(1, j)
        moments[0] = moments[0] + fold(field * source)
    for stage in (1, 2):
        for j in range(CHUNKS):
            get_halo(stage, j)
            span = slice(j * width, (j + 1) * width)
            image = None
            for i, name in enumerate(names):
                term = coefs[i, :, span] * near(stage, j, name)
                image = term if image is None else image + term
            field = inv_ref[:, span] * image
            put_field(stage + 1, j, field)
            send_field(stage + 1, j)
            moments[2 * stage - 1] = moments[2 * stage - 1] + fold(here(stage, j) * image)
            moments[2 * stage] = moments[2 * stage] + fold(field * image)
        deliver(stage - 1)
    for j in range(CHUNKS):
        get_halo(3, j)
        span = slice(j * width, (j + 1) * width)
        side = "below" if j < CHUNKS // 2 else "above"
        image = None
        for name in ("west", "north", side):
            term = coefs[names.index(name), :, span] * near(3, j, name)
            image = term if image is None else image + term
        moments[5] = moments[5] + fold(here(3, j) * image)
    moments[5] = 2.0 * moments[5]

    sums = [jnp.sum(m, axis=0, keepdims=True) for m in moments]
    red_layer[layer] = jnp.concatenate(sums + [jnp.zeros((2, 128), jnp.float32)], axis=0)
    repeat(1, n_layer, lambda d: layer_sum_copy(d).start())
    deliver(2)
    repeat(1, n_layer, lambda d: layer_sum_copy(d).wait_recv())
    red_slab[slab] = sum(red_layer[i] for i in range(n_layer))
    repeat(1, n_slab, lambda d: slab_sum_copy(d).start())
    for stage in range(4):
        for j in range(CHUNKS):
            for direction in range(4):
                if sent_with(stage, direction, j):

                    @pl.when(sends_to[direction] & wanted(stage, direction, j, layer))
                    def _():
                        halo_copy(stage, direction, j).wait_send()
    for k in range(ITERS - 1):
        repeat(1, n_pair * n_slab, lambda n: tile_copy(k, n).wait_recv())
        repeat(1, n_pair * n_slab, lambda n: tile_copy(k, n).wait_send())
    repeat(1, n_layer, lambda d: layer_sum_copy(d).wait_send())
    repeat(1, n_slab, lambda d: slab_sum_copy(d).wait_recv())
    total = jnp.sum(sum(red_slab[i] for i in range(n_slab)), axis=1, keepdims=True)
    scales = [2.0 * c for c in cg_coefficients([total[k : k + 1] for k in range(6)])]

    for j in range(CHUNKS):
        value = scales[0] * here(1, j) + scales[1] * here(2, j) + scales[2] * here(3, j)
        x_buf[:, j * width : (j + 1) * width] = value
    x_copy = pltpu.make_async_copy(x_buf, x_out.at[0], local_sem.at[0])
    x_copy.start()

    repeat(1, n_pair * n_slab, lambda n: tile_copy(ITERS - 1, n).wait_recv())

    def combine(i, carry):
        value = None
        for k in range(ITERS):
            term = scales[k] * sum(tile_recv[k, p, i] for p in range(n_pair))
            value = term if value is None else value + term
        tiles[i] = value
        return carry

    lax.fori_loop(0, n_slab, combine, 0)
    if tile_rows == 1:
        turned = jnp.transpose(tiles[...].reshape(TILE, TILE))
        for k in range(owned_count):
            g_buf[k] = turned[k * strip : (k + 1) * strip]
    else:
        count = jnp.int32(0)
        picked = [jnp.int32(0)] * owned_count
        for r in range(tile_rows):
            for t in range(tiles_across):
                mine = owner_ref[r, t] == slab
                picked = [jnp.where(mine & (count == k), r, p) for k, p in enumerate(picked)]
                count = jnp.where(mine, count + 1, count)
        for k in range(owned_count):
            block = tiles[pl.ds(picked[k] * per_tile, per_tile)].reshape(TILE, TILE)
            g_buf[k] = jnp.transpose(block)[0:strip]

    g_copy = pltpu.make_async_copy(g_buf, g_out, local_sem.at[1])
    g_copy.start()

    repeat(1, n_slab, lambda d: slab_sum_copy(d).wait_send())
    repeat(1, n_pair * n_slab, lambda n: tile_copy(ITERS - 1, n).wait_send())
    x_copy.wait()
    g_copy.wait()


def per_device(adjoint_source, conductivity, tile_owner):
    n_slab, n_layer = lax.axis_size("slab"), lax.axis_size("layer")
    depth, rows, cols = adjoint_source.shape
    owned = tile_owner.shape[0] * tile_owner.shape[1] // n_slab
    strip = TILE // n_layer
    width = cols // CHUNKS
    f32 = jnp.float32
    return pl.pallas_call(
        functools.partial(kernel, n_slab, n_layer),
        out_shape=(
            jax.ShapeDtypeStruct((depth, rows, cols), f32),
            jax.ShapeDtypeStruct((owned, strip, TILE), f32),
        ),
        in_specs=[pl.BlockSpec(memory_space=pltpu.HBM)] * 3,
        out_specs=(pl.BlockSpec(memory_space=pl.ANY), pl.BlockSpec(memory_space=pl.ANY)),
        scratch_shapes=[
            pltpu.VMEM((rows, cols), f32),
            pltpu.SMEM(tile_owner.shape, jnp.int32),
            pltpu.VMEM((4, rows + 16, cols + 2 * PAD), f32),
            pltpu.VMEM((6, rows, cols), f32),
            pltpu.VMEM((rows, cols), f32),
            pltpu.VMEM((4, 2, rows, cols), f32),
            pltpu.VMEM((4, 2, ROW_CHUNKS, 1, cols // ROW_CHUNKS), f32),
            pltpu.VMEM((4, 2, ROW_CHUNKS, 1, cols // ROW_CHUNKS), f32),
            pltpu.VMEM((n_layer, 8, 128), f32),
            pltpu.VMEM((n_slab, 8, 128), f32),
            pltpu.VMEM((rows, cols), f32),
            pltpu.VMEM((cols // TILE, rows, TILE), f32),
            pltpu.VMEM((ITERS, n_layer // 2, n_slab, rows, TILE), f32),
            pltpu.VMEM((ITERS, n_layer // 2, n_slab, rows, TILE), f32),
            pltpu.VMEM((n_slab, rows, TILE), f32),
            pltpu.VMEM((owned, strip, TILE), f32),
            pltpu.SMEM((n_slab,), jnp.int32),
            pltpu.SemaphoreType.DMA((4, 4, CHUNKS)),
            pltpu.SemaphoreType.DMA((4, 4, CHUNKS)),
            pltpu.SemaphoreType.DMA((2, max(n_slab, n_layer))),
            pltpu.SemaphoreType.DMA((2, max(n_slab, n_layer))),
            pltpu.SemaphoreType.DMA((ITERS, n_layer // 2 * n_slab)),
            pltpu.SemaphoreType.DMA((ITERS, n_layer // 2 * n_slab)),
            pltpu.SemaphoreType.DMA((3,)),
        ],
        compiler_params=pltpu.CompilerParams(
            collective_id=0, has_side_effects=True, vmem_limit_bytes=48 * 1024 * 1024
        ),
        name="stack_cg",
    )(*[pltpu.with_memory_space_constraint(v, pltpu.HBM) for v in (adjoint_source, conductivity, tile_owner)])


def solution(mesh):
    placed = (P("layer", "slab", None), P("layer", "slab", None), P())
    return jax.shard_map(
        per_device,
        mesh=mesh,
        in_specs=placed,
        out_specs=(P("layer", "slab", None), P("slab", "layer", None)),
        check_vma=False,
    )
```

```python
import functools

import jax
import jax.numpy as jnp
from jax import lax
from jax.experimental import pallas as pl
from jax.experimental.pallas import tpu as pltpu
from jax.sharding import PartitionSpec as P

TILE = 128
ITERS = 3
CHUNKS = 4
ROW_CHUNKS = 2
PAD = 128
MESH = pl.DeviceIdType.MESH


def fold(value):
    rows = sum(value[i : i + 8] for i in range(0, value.shape[0], 8))
    return sum(rows[:, i : i + 128] for i in range(0, value.shape[1], 128))


def cg_coefficients(mu):
    def inner(a, b):
        total = None
        for k in range(len(a) + len(b) - 1):
            coef = None
            for i in range(len(a)):
                if 0 <= k - i < len(b):
                    term = a[i] * b[k - i]
                    coef = term if coef is None else coef + term
            total = coef * mu[k] if total is None else total + coef * mu[k]
        return total

    def axpy(a, s, b):
        out = []
        for i in range(max(len(a), len(b))):
            if i >= len(b):
                out.append(a[i])
            elif i >= len(a):
                out.append(s * b[i])
            else:
                out.append(a[i] + s * b[i])
        return out

    one = jnp.ones_like(mu[0])
    zero = jnp.zeros_like(mu[0])
    sol, res, direction, now = [zero], [one], [one], mu[0]
    for iteration in range(ITERS):
        image = axpy(direction + [zero], -one, [zero] + direction)
        step = now / inner(direction, image)
        sol = axpy(sol, step, direction)
        if iteration + 1 < ITERS:
            res = axpy(res, -step, image)
            new = inner(res, res)
            direction = axpy(res, new / now, direction)
            now = new
    return sol


def kernel(
    n_slab,
    n_layer,
    src_hbm,
    cond_hbm,
    owner_hbm,
    x_out,
    g_out,
    src_ref,
    owner_ref,
    fields,
    coefs,
    inv_ref,
    layer_halo,
    row_send,
    row_recv,
    red_layer,
    red_slab,
    x_buf,
    x_tiles,
    tile_send,
    tile_recv,
    tiles,
    g_buf,
    table,
    halo_ssem,
    halo_rsem,
    red_ssem,
    red_rsem,
    tile_ssem,
    tile_rsem,
    local_sem,
):
    slab = lax.axis_index("slab")
    layer = lax.axis_index("layer")
    rows, cols = src_ref.shape
    width = cols // CHUNKS
    per_row = CHUNKS // ROW_CHUNKS
    top, bottom = 8, 8 + rows
    tile_rows, tiles_across = owner_ref.shape
    strip = TILE // n_layer
    capacity = max(1, tiles_across // n_slab)
    owned_count = g_out.shape[0]
    per_tile = TILE // rows

    pair, core = layer // 2, layer % 2
    n_pair = n_layer // 2

    def turn(me, d, count):
        return lax.rem(me + d, count)

    def layer_peer(d):
        return {"layer": turn(layer, d, n_layer)}

    def slab_peer(d):
        return {"slab": turn(slab, d, n_slab)}

    def tile_peer(n):
        to_pair, to_slab = turn(pair, n // n_slab, n_pair), turn(slab, n % n_slab, n_slab)
        return to_pair, to_slab, {"layer": 2 * to_pair + core, "slab": to_slab}

    def repeat(start, stop, body):
        if stop - start <= 32:
            for n in range(start, stop):
                body(n)
        else:
            lax.fori_loop(start, stop, lambda n, carry: (body(n), carry)[1], 0)

    barrier = pltpu.get_barrier_semaphore()

    def greet(device):
        pl.semaphore_signal(barrier, inc=1, device_id=device, device_id_type=MESH)

    n_greet = 0
    for d in range(1, n_layer):
        if d % 2 == 1:
            greet(layer_peer(d))
            n_greet += 1
    repeat(1, n_pair * n_slab, lambda n: greet(tile_peer(n)[2]))
    n_greet += n_pair * n_slab - 1

    cond_copy = pltpu.make_async_copy(
        cond_hbm.at[0], fields.at[0, pl.ds(top, rows), pl.ds(PAD, cols)], local_sem.at[0]
    )
    src_copy = pltpu.make_async_copy(src_hbm.at[0], src_ref, local_sem.at[1])
    owner_copy = pltpu.make_async_copy(owner_hbm, owner_ref, local_sem.at[2])
    cond_copy.start()
    src_copy.start()
    owner_copy.start()

    for s in range(4):
        fields[s, :, 0:PAD] = jnp.zeros((rows + 16, PAD), jnp.float32)
        fields[s, :, PAD + cols :] = jnp.zeros((rows + 16, PAD), jnp.float32)
    for d, axis_end in enumerate((layer == 0, layer == n_layer - 1)):

        @pl.when(axis_end)
        def _():
            for s in range(4):
                layer_halo[s, d] = jnp.zeros((rows, cols), jnp.float32)

    for d, axis_end in enumerate((slab == 0, slab == n_slab - 1)):

        @pl.when(axis_end)
        def _():
            for s in range(4):
                for j in range(ROW_CHUNKS):
                    row_recv[s, d, j] = jnp.zeros((1, cols // ROW_CHUNKS), jnp.float32)

    sends_to = (layer < n_layer - 1, layer > 0, slab < n_slab - 1, slab > 0)
    gets_from = (layer > 0, layer < n_layer - 1, slab > 0, slab < n_slab - 1)
    target = (
        {"layer": lax.rem(layer + 1, n_layer)},
        {"layer": lax.rem(layer + n_layer - 1, n_layer)},
        {"slab": lax.rem(slab + 1, n_slab)},
        {"slab": lax.rem(slab + n_slab - 1, n_slab)},
    )

    def used(stage, direction, j):
        if stage < 3:
            return True
        return direction < 3

    def wanted(stage, direction, j, sender_layer):
        if stage == 3 and direction == 0 and j >= CHUNKS // 2:
            return sender_layer % 2 == 0
        if stage == 3 and direction == 1 and j < CHUNKS // 2:
            return sender_layer % 2 == 1
        return True

    def halo_copy(stage, direction, j):
        span = pl.ds(j * width, width)
        slot = j if direction < 2 else j // per_row
        if direction < 2:
            source = fields.at[stage, pl.ds(top, rows), pl.ds(PAD + j * width, width)]
            dest = layer_halo.at[stage, direction, :, span]
        else:
            source = row_send.at[stage, direction - 2, j // per_row]
            dest = row_recv.at[stage, direction - 2, j // per_row]
        return pltpu.make_async_remote_copy(
            src_ref=source,
            dst_ref=dest,
            send_sem=halo_ssem.at[stage, direction, slot],
            recv_sem=halo_rsem.at[stage, direction, slot],
            device_id=target[direction],
            device_id_type=MESH,
        )

    def put_field(stage, j, value):
        fields[stage, top:bottom, PAD + j * width : PAD + (j + 1) * width] = value
        part = slice((j % per_row) * width, (j % per_row + 1) * width)
        row_send[stage, 0, j // per_row, :, part] = value[rows - 1 : rows]
        row_send[stage, 1, j // per_row, :, part] = value[0:1]

    def sent_with(stage, direction, j):
        return used(stage, direction, j) and (direction < 2 or j % per_row == per_row - 1)

    def got_with(stage, direction, j):
        return used(stage, direction, j) and (direction < 2 or j % per_row == 0)

    def send_field(stage, j):
        for direction in range(4):
            if sent_with(stage, direction, j):

                @pl.when(sends_to[direction] & wanted(stage, direction, j, layer))
                def _():
                    halo_copy(stage, direction, j).start()

    def get_halo(stage, j):
        for direction in range(4):
            if got_with(stage, direction, j):

                @pl.when(gets_from[direction] & wanted(stage, direction, j, layer + 1))
                def _():
                    halo_copy(stage, direction, j).wait_recv()

        span = slice(PAD + j * width, PAD + (j + 1) * width)
        part = slice((j % per_row) * width, (j % per_row + 1) * width)
        fields[stage, top - 1 : top, span] = row_recv[stage, 0, j // per_row, :, part]
        if stage < 3:
            fields[stage, bottom : bottom + 1, span] = row_recv[stage, 1, j // per_row, :, part]

    def near(stage, j, which):
        c0 = j * width
        if which == "west":
            ext = fields[stage, top:bottom, c0 : c0 + width + 2 * PAD]
            return pltpu.roll(ext, 1, 1)[:, PAD : PAD + width]
        if which == "east":
            ext = fields[stage, top:bottom, c0 : c0 + width + 2 * PAD]
            return pltpu.roll(ext, width + 2 * PAD - 1, 1)[:, PAD : PAD + width]
        span = slice(PAD + c0, PAD + c0 + width)
        if which == "north":
            return fields[stage, top - 1 : bottom - 1, span]
        if which == "south":
            return fields[stage, top + 1 : bottom + 1, span]
        return layer_halo[stage, 0 if which == "below" else 1, :, c0 : c0 + width]

    names = ("west", "east", "north", "south", "below", "above")

    def here(stage, j):
        return fields[stage, top:bottom, PAD + j * width : PAD + (j + 1) * width]

    cond_copy.wait()
    for j in range(CHUNKS):
        part = slice((j % per_row) * width, (j % per_row + 1) * width)
        span = slice(PAD + j * width, PAD + (j + 1) * width)
        row_send[0, 0, j // per_row, :, part] = fields[0, bottom - 1 : bottom, span]
        row_send[0, 1, j // per_row, :, part] = fields[0, top : top + 1, span]
    pl.semaphore_wait(barrier, n_greet)
    for j in range(CHUNKS):
        send_field(0, j)

    owner_copy.wait()
    my_row = slab // per_tile

    def list_tiles(owner, carry):
        packed = jnp.int32(0)
        for t in range(tiles_across):
            packed = jnp.where(owner_ref[my_row, t] == owner, packed * 256 + t, packed)
        table[owner] = packed
        return carry

    lax.fori_loop(0, n_slab, list_tiles, 0)

    def layer_sum_copy(d):
        return pltpu.make_async_remote_copy(
            src_ref=red_layer.at[layer],
            dst_ref=red_layer.at[layer],
            send_sem=red_ssem.at[0, d],
            recv_sem=red_rsem.at[0, d],
            device_id=layer_peer(d),
            device_id_type=MESH,
        )

    def slab_sum_copy(d):
        return pltpu.make_async_remote_copy(
            src_ref=red_slab.at[slab],
            dst_ref=red_slab.at[slab],
            send_sem=red_ssem.at[1, d],
            recv_sem=red_rsem.at[1, d],
            device_id=slab_peer(d),
            device_id_type=MESH,
        )

    def tile_copy(k, n):
        to_pair, to_slab, device = tile_peer(n)
        return pltpu.make_async_remote_copy(
            src_ref=tile_send.at[k, to_pair, to_slab],
            dst_ref=tile_recv.at[k, pair, slab],
            send_sem=tile_ssem.at[k, n],
            recv_sem=tile_rsem.at[k, n],
            device_id=device,
            device_id_type=MESH,
        )

    lane = lax.broadcasted_iota(jnp.int32, (rows, TILE), 1) // strip

    def deliver(k):
        for j in range(CHUNKS):
            value = here(k + 1, j) + layer_halo[k + 1, 1 - core, :, j * width : (j + 1) * width]
            for t in range(width // TILE):
                x_tiles[j * (width // TILE) + t] = value[:, t * TILE : (t + 1) * TILE]

        def pack(owner):
            packed = table[owner]
            pieces = [None] * n_pair
            for q in range(capacity):
                t = lax.shift_right_logical(packed, 8 * (capacity - 1 - q)) & 255
                tile = x_tiles[t]
                tile = jnp.where(core == 1, pltpu.roll(tile, TILE - strip, 1), tile)
                for p in range(n_pair):
                    shift = ((q - 2 * p) * strip) % TILE
                    moved = tile if shift == 0 else pltpu.roll(tile, shift, 1)
                    pieces[p] = moved if q == 0 else jnp.where(lane == q, moved, pieces[p])
            for p in range(n_pair):
                tile_send[k, p, owner] = pieces[p]

        repeat(0, n_slab, pack)
        repeat(1, n_pair * n_slab, lambda n: tile_copy(k, n).start())
        tile_recv[k, pair, slab] = tile_send[k, pair, slab]

    src_copy.wait()
    moments = [jnp.zeros((8, 128), jnp.float32) for _ in range(6)]
    for j in range(CHUNKS):
        get_halo(0, j)
        span = slice(j * width, (j + 1) * width)
        cond = here(0, j)
        diagonal = None
        for i, name in enumerate(names):
            face = cond + near(0, j, name)
            coefs[i, :, span] = face
            diagonal = face if diagonal is None else diagonal + face
        inverse = 1.0 / diagonal
        inv_ref[:, span] = inverse
        source = src_ref[:, span]
        field = source * inverse
        put_field(1, j, field)
        send_field(1, j)
        moments[0] = moments[0] + fold(field * source)
    for stage in (1, 2):
        for j in range(CHUNKS):
            get_halo(stage, j)
            span = slice(j * width, (j + 1) * width)
            image = None
            for i, name in enumerate(names):
                term = coefs[i, :, span] * near(stage, j, name)
                image = term if image is None else image + term
            field = inv_ref[:, span] * image
            put_field(stage + 1, j, field)
            send_field(stage + 1, j)
            moments[2 * stage - 1] = moments[2 * stage - 1] + fold(here(stage, j) * image)
            moments[2 * stage] = moments[2 * stage] + fold(field * image)
        deliver(stage - 1)
    for j in range(CHUNKS):
        get_halo(3, j)
        span = slice(j * width, (j + 1) * width)
        side = "below" if j < CHUNKS // 2 else "above"
        image = None
        for name in ("west", "north", side):
            term = coefs[names.index(name), :, span] * near(3, j, name)
            image = term if image is None else image + term
        moments[5] = moments[5] + fold(here(3, j) * image)
    moments[5] = 2.0 * moments[5]

    sums = [jnp.sum(m, axis=0, keepdims=True) for m in moments]
    red_layer[layer] = jnp.concatenate(sums + [jnp.zeros((2, 128), jnp.float32)], axis=0)
    repeat(1, n_layer, lambda d: layer_sum_copy(d).start())
    deliver(2)
    repeat(1, n_layer, lambda d: layer_sum_copy(d).wait_recv())
    red_slab[slab] = sum(red_layer[i] for i in range(n_layer))
    repeat(1, n_slab, lambda d: slab_sum_copy(d).start())
    for stage in range(4):
        for j in range(CHUNKS):
            for direction in range(4):
                if sent_with(stage, direction, j):

                    @pl.when(sends_to[direction] & wanted(stage, direction, j, layer))
                    def _():
                        halo_copy(stage, direction, j).wait_send()
    for k in range(ITERS - 1):
        repeat(1, n_pair * n_slab, lambda n: tile_copy(k, n).wait_recv())
        repeat(1, n_pair * n_slab, lambda n: tile_copy(k, n).wait_send())
    repeat(1, n_layer, lambda d: layer_sum_copy(d).wait_send())
    repeat(1, n_slab, lambda d: slab_sum_copy(d).wait_recv())
    total = jnp.sum(sum(red_slab[i] for i in range(n_slab)), axis=1, keepdims=True)
    scales = [2.0 * c for c in cg_coefficients([total[k : k + 1] for k in range(6)])]

    for j in range(CHUNKS):
        value = scales[0] * here(1, j) + scales[1] * here(2, j) + scales[2] * here(3, j)
        x_buf[:, j * width : (j + 1) * width] = value
    x_copy = pltpu.make_async_copy(x_buf, x_out.at[0], local_sem.at[0])
    x_copy.start()

    repeat(1, n_pair * n_slab, lambda n: tile_copy(ITERS - 1, n).wait_recv())

    def combine(i):
        value = None
        for k in range(ITERS):
            term = scales[k] * sum(tile_recv[k, p, i] for p in range(n_pair))
            value = term if value is None else value + term
        tiles[i] = value

    repeat(0, n_slab, combine)
    if tile_rows == 1:
        turned = jnp.transpose(tiles[...].reshape(TILE, TILE))
        for k in range(owned_count):
            g_buf[k] = turned[k * strip : (k + 1) * strip]
    else:
        count = jnp.int32(0)
        picked = [jnp.int32(0)] * owned_count
        for r in range(tile_rows):
            for t in range(tiles_across):
                mine = owner_ref[r, t] == slab
                picked = [jnp.where(mine & (count == k), r, p) for k, p in enumerate(picked)]
                count = jnp.where(mine, count + 1, count)
        for k in range(owned_count):
            block = tiles[pl.ds(picked[k] * per_tile, per_tile)].reshape(TILE, TILE)
            g_buf[k] = jnp.transpose(block)[0:strip]

    g_copy = pltpu.make_async_copy(g_buf, g_out, local_sem.at[1])
    g_copy.start()

    repeat(1, n_slab, lambda d: slab_sum_copy(d).wait_send())
    repeat(1, n_pair * n_slab, lambda n: tile_copy(ITERS - 1, n).wait_send())
    x_copy.wait()
    g_copy.wait()


def per_device(adjoint_source, conductivity, tile_owner):
    n_slab, n_layer = lax.axis_size("slab"), lax.axis_size("layer")
    depth, rows, cols = adjoint_source.shape
    owned = tile_owner.shape[0] * tile_owner.shape[1] // n_slab
    strip = TILE // n_layer
    width = cols // CHUNKS
    f32 = jnp.float32
    return pl.pallas_call(
        functools.partial(kernel, n_slab, n_layer),
        out_shape=(
            jax.ShapeDtypeStruct((depth, rows, cols), f32),
            jax.ShapeDtypeStruct((owned, strip, TILE), f32),
        ),
        in_specs=[pl.BlockSpec(memory_space=pltpu.HBM)] * 3,
        out_specs=(pl.BlockSpec(memory_space=pl.ANY), pl.BlockSpec(memory_space=pl.ANY)),
        scratch_shapes=[
            pltpu.VMEM((rows, cols), f32),
            pltpu.SMEM(tile_owner.shape, jnp.int32),
            pltpu.VMEM((4, rows + 16, cols + 2 * PAD), f32),
            pltpu.VMEM((6, rows, cols), f32),
            pltpu.VMEM((rows, cols), f32),
            pltpu.VMEM((4, 2, rows, cols), f32),
            pltpu.VMEM((4, 2, ROW_CHUNKS, 1, cols // ROW_CHUNKS), f32),
            pltpu.VMEM((4, 2, ROW_CHUNKS, 1, cols // ROW_CHUNKS), f32),
            pltpu.VMEM((n_layer, 8, 128), f32),
            pltpu.VMEM((n_slab, 8, 128), f32),
            pltpu.VMEM((rows, cols), f32),
            pltpu.VMEM((cols // TILE, rows, TILE), f32),
            pltpu.VMEM((ITERS, n_layer // 2, n_slab, rows, TILE), f32),
            pltpu.VMEM((ITERS, n_layer // 2, n_slab, rows, TILE), f32),
            pltpu.VMEM((n_slab, rows, TILE), f32),
            pltpu.VMEM((owned, strip, TILE), f32),
            pltpu.SMEM((n_slab,), jnp.int32),
            pltpu.SemaphoreType.DMA((4, 4, CHUNKS)),
            pltpu.SemaphoreType.DMA((4, 4, CHUNKS)),
            pltpu.SemaphoreType.DMA((2, max(n_slab, n_layer))),
            pltpu.SemaphoreType.DMA((2, max(n_slab, n_layer))),
            pltpu.SemaphoreType.DMA((ITERS, n_layer // 2 * n_slab)),
            pltpu.SemaphoreType.DMA((ITERS, n_layer // 2 * n_slab)),
            pltpu.SemaphoreType.DMA((3,)),
        ],
        compiler_params=pltpu.CompilerParams(
            collective_id=0, has_side_effects=True, vmem_limit_bytes=48 * 1024 * 1024
        ),
        name="stack_cg",
    )(*[pltpu.with_memory_space_constraint(v, pltpu.HBM) for v in (adjoint_source, conductivity, tile_owner)])


def solution(mesh):
    placed = (P("layer", "slab", None), P("layer", "slab", None), P())
    return jax.shard_map(
        per_device,
        mesh=mesh,
        in_specs=placed,
        out_specs=(P("layer", "slab", None), P("slab", "layer", None)),
        check_vma=False,
    )
```

```python
import functools

import jax
import jax.numpy as jnp
from jax import lax
from jax.experimental import pallas as pl
from jax.experimental.pallas import tpu as pltpu
from jax.sharding import PartitionSpec as P

TILE = 128
ITERS = 3
CHUNKS = 4
ROW_CHUNKS = 2
PAD = 128
MESH = pl.DeviceIdType.MESH


def fold(value):
    rows = sum(value[i : i + 8] for i in range(0, value.shape[0], 8))
    return sum(rows[:, i : i + 128] for i in range(0, value.shape[1], 128))


def cg_coefficients(mu):
    def inner(a, b):
        total = None
        for k in range(len(a) + len(b) - 1):
            coef = None
            for i in range(len(a)):
                if 0 <= k - i < len(b):
                    term = a[i] * b[k - i]
                    coef = term if coef is None else coef + term
            total = coef * mu[k] if total is None else total + coef * mu[k]
        return total

    def axpy(a, s, b):
        out = []
        for i in range(max(len(a), len(b))):
            if i >= len(b):
                out.append(a[i])
            elif i >= len(a):
                out.append(s * b[i])
            else:
                out.append(a[i] + s * b[i])
        return out

    one = jnp.ones_like(mu[0])
    zero = jnp.zeros_like(mu[0])
    sol, res, direction, now = [zero], [one], [one], mu[0]
    for iteration in range(ITERS):
        image = axpy(direction + [zero], -one, [zero] + direction)
        step = now / inner(direction, image)
        sol = axpy(sol, step, direction)
        if iteration + 1 < ITERS:
            res = axpy(res, -step, image)
            new = inner(res, res)
            direction = axpy(res, new / now, direction)
            now = new
    return sol


def kernel(
    n_slab,
    n_layer,
    src_hbm,
    cond_hbm,
    owner_hbm,
    x_out,
    g_out,
    src_ref,
    owner_ref,
    fields,
    coefs,
    inv_ref,
    layer_halo,
    row_send,
    row_recv,
    sums,
    x_buf,
    x_tiles,
    tile_send,
    tile_recv,
    tiles,
    g_buf,
    table,
    halo_ssem,
    halo_rsem,
    sum_ssem,
    sum_rsem,
    tile_ssem,
    tile_rsem,
    local_sem,
):
    slab = lax.axis_index("slab")
    layer = lax.axis_index("layer")
    rows, cols = src_ref.shape
    width = cols // CHUNKS
    per_row = CHUNKS // ROW_CHUNKS
    top, bottom = 8, 8 + rows
    tile_rows, tiles_across = owner_ref.shape
    strip = TILE // n_layer
    capacity = max(1, tiles_across // n_slab)
    owned_count = g_out.shape[0]
    per_tile = TILE // rows

    pair, core = layer // 2, layer % 2
    n_pair = n_layer // 2

    def turn(me, d, count):
        return lax.rem(me + d, count)

    def any_peer(n):
        return {"layer": turn(layer, n // n_slab, n_layer), "slab": turn(slab, n % n_slab, n_slab)}

    def tile_peer(n):
        to_pair, to_slab = turn(pair, n // n_slab, n_pair), turn(slab, n % n_slab, n_slab)
        return to_pair, to_slab, {"layer": 2 * to_pair + core, "slab": to_slab}

    def repeat(start, stop, body):
        if stop - start <= 32:
            for n in range(start, stop):
                body(n)
        else:
            lax.fori_loop(start, stop, lambda n, carry: (body(n), carry)[1], 0)

    barrier = pltpu.get_barrier_semaphore()

    def greet(device):
        pl.semaphore_signal(barrier, inc=1, device_id=device, device_id_type=MESH)

    n_greet = n_layer * n_slab - 1
    repeat(1, n_greet + 1, lambda n: greet(any_peer(n)))

    cond_copy = pltpu.make_async_copy(
        cond_hbm.at[0], fields.at[0, pl.ds(top, rows), pl.ds(PAD, cols)], local_sem.at[0]
    )
    src_copy = pltpu.make_async_copy(src_hbm.at[0], src_ref, local_sem.at[1])
    owner_copy = pltpu.make_async_copy(owner_hbm, owner_ref, local_sem.at[2])
    cond_copy.start()
    src_copy.start()
    owner_copy.start()

    for s in range(4):
        fields[s, :, 0:PAD] = jnp.zeros((rows + 16, PAD), jnp.float32)
        fields[s, :, PAD + cols :] = jnp.zeros((rows + 16, PAD), jnp.float32)
    for d, axis_end in enumerate((layer == 0, layer == n_layer - 1)):

        @pl.when(axis_end)
        def _():
            for s in range(4):
                layer_halo[s, d] = jnp.zeros((rows, cols), jnp.float32)

    for d, axis_end in enumerate((slab == 0, slab == n_slab - 1)):

        @pl.when(axis_end)
        def _():
            for s in range(4):
                for j in range(ROW_CHUNKS):
                    row_recv[s, d, j] = jnp.zeros((1, cols // ROW_CHUNKS), jnp.float32)

    sends_to = (layer < n_layer - 1, layer > 0, slab < n_slab - 1, slab > 0)
    gets_from = (layer > 0, layer < n_layer - 1, slab > 0, slab < n_slab - 1)
    target = (
        {"layer": lax.rem(layer + 1, n_layer)},
        {"layer": lax.rem(layer + n_layer - 1, n_layer)},
        {"slab": lax.rem(slab + 1, n_slab)},
        {"slab": lax.rem(slab + n_slab - 1, n_slab)},
    )

    def used(stage, direction, j):
        if stage < 3:
            return True
        return direction < 3

    def wanted(stage, direction, j, sender_layer):
        if stage == 3 and direction == 0 and j >= CHUNKS // 2:
            return sender_layer % 2 == 0
        if stage == 3 and direction == 1 and j < CHUNKS // 2:
            return sender_layer % 2 == 1
        return True

    def halo_copy(stage, direction, j):
        span = pl.ds(j * width, width)
        slot = j if direction < 2 else j // per_row
        if direction < 2:
            source = fields.at[stage, pl.ds(top, rows), pl.ds(PAD + j * width, width)]
            dest = layer_halo.at[stage, direction, :, span]
        else:
            source = row_send.at[stage, direction - 2, j // per_row]
            dest = row_recv.at[stage, direction - 2, j // per_row]
        return pltpu.make_async_remote_copy(
            src_ref=source,
            dst_ref=dest,
            send_sem=halo_ssem.at[stage, direction, slot],
            recv_sem=halo_rsem.at[stage, direction, slot],
            device_id=target[direction],
            device_id_type=MESH,
        )

    def put_field(stage, j, value):
        fields[stage, top:bottom, PAD + j * width : PAD + (j + 1) * width] = value
        part = slice((j % per_row) * width, (j % per_row + 1) * width)
        row_send[stage, 0, j // per_row, :, part] = value[rows - 1 : rows]
        row_send[stage, 1, j // per_row, :, part] = value[0:1]

    def sent_with(stage, direction, j):
        return used(stage, direction, j) and (direction < 2 or j % per_row == per_row - 1)

    def got_with(stage, direction, j):
        return used(stage, direction, j) and (direction < 2 or j % per_row == 0)

    def send_field(stage, j):
        for direction in range(4):
            if sent_with(stage, direction, j):

                @pl.when(sends_to[direction] & wanted(stage, direction, j, layer))
                def _():
                    halo_copy(stage, direction, j).start()

    def get_halo(stage, j):
        for direction in range(4):
            if got_with(stage, direction, j):

                @pl.when(gets_from[direction] & wanted(stage, direction, j, layer + 1))
                def _():
                    halo_copy(stage, direction, j).wait_recv()

        span = slice(PAD + j * width, PAD + (j + 1) * width)
        part = slice((j % per_row) * width, (j % per_row + 1) * width)
        fields[stage, top - 1 : top, span] = row_recv[stage, 0, j // per_row, :, part]
        if stage < 3:
            fields[stage, bottom : bottom + 1, span] = row_recv[stage, 1, j // per_row, :, part]

    def near(stage, j, which):
        c0 = j * width
        if which == "west":
            ext = fields[stage, top:bottom, c0 : c0 + width + 2 * PAD]
            return pltpu.roll(ext, 1, 1)[:, PAD : PAD + width]
        if which == "east":
            ext = fields[stage, top:bottom, c0 : c0 + width + 2 * PAD]
            return pltpu.roll(ext, width + 2 * PAD - 1, 1)[:, PAD : PAD + width]
        span = slice(PAD + c0, PAD + c0 + width)
        if which == "north":
            return fields[stage, top - 1 : bottom - 1, span]
        if which == "south":
            return fields[stage, top + 1 : bottom + 1, span]
        return layer_halo[stage, 0 if which == "below" else 1, :, c0 : c0 + width]

    names = ("west", "east", "north", "south", "below", "above")

    def here(stage, j):
        return fields[stage, top:bottom, PAD + j * width : PAD + (j + 1) * width]

    cond_copy.wait()
    for j in range(CHUNKS):
        part = slice((j % per_row) * width, (j % per_row + 1) * width)
        span = slice(PAD + j * width, PAD + (j + 1) * width)
        row_send[0, 0, j // per_row, :, part] = fields[0, bottom - 1 : bottom, span]
        row_send[0, 1, j // per_row, :, part] = fields[0, top : top + 1, span]
    pl.semaphore_wait(barrier, n_greet)
    for j in range(CHUNKS):
        send_field(0, j)

    owner_copy.wait()
    my_row = slab // per_tile

    def list_tiles(owner, carry):
        packed = jnp.int32(0)
        for t in range(tiles_across):
            packed = jnp.where(owner_ref[my_row, t] == owner, packed * 256 + t, packed)
        table[owner] = packed
        return carry

    lax.fori_loop(0, n_slab, list_tiles, 0)

    def sum_copy(n):
        return pltpu.make_async_remote_copy(
            src_ref=sums.at[layer * n_slab + slab],
            dst_ref=sums.at[layer * n_slab + slab],
            send_sem=sum_ssem,
            recv_sem=sum_rsem,
            device_id=any_peer(n),
            device_id_type=MESH,
        )

    others = pl.ds(0, n_layer * n_slab - 1)
    all_sums = pltpu.make_async_remote_copy(
        src_ref=sums.at[others],
        dst_ref=sums.at[others],
        send_sem=sum_ssem,
        recv_sem=sum_rsem,
        device_id=any_peer(1),
        device_id_type=MESH,
    )

    def tile_copy(k, n):
        to_pair, to_slab, device = tile_peer(n)
        return pltpu.make_async_remote_copy(
            src_ref=tile_send.at[k, to_pair, to_slab],
            dst_ref=tile_recv.at[k, pair, slab],
            send_sem=tile_ssem.at[k, n],
            recv_sem=tile_rsem.at[k, n],
            device_id=device,
            device_id_type=MESH,
        )

    lane = lax.broadcasted_iota(jnp.int32, (rows, TILE), 1) // strip

    def deliver(k):
        for j in range(CHUNKS):
            value = here(k + 1, j) + layer_halo[k + 1, 1 - core, :, j * width : (j + 1) * width]
            for t in range(width // TILE):
                x_tiles[j * (width // TILE) + t] = value[:, t * TILE : (t + 1) * TILE]

        def pack(owner):
            packed = table[owner]
            pieces = [None] * n_pair
            for q in range(capacity):
                t = lax.shift_right_logical(packed, 8 * (capacity - 1 - q)) & 255
                tile = x_tiles[t]
                tile = jnp.where(core == 1, pltpu.roll(tile, TILE - strip, 1), tile)
                for p in range(n_pair):
                    shift = ((q - 2 * p) * strip) % TILE
                    moved = tile if shift == 0 else pltpu.roll(tile, shift, 1)
                    pieces[p] = moved if q == 0 else jnp.where(lane == q, moved, pieces[p])
            for p in range(n_pair):
                tile_send[k, p, owner] = pieces[p]

        repeat(0, n_slab, pack)
        repeat(1, n_pair * n_slab, lambda n: tile_copy(k, n).start())
        tile_recv[k, pair, slab] = tile_send[k, pair, slab]

    src_copy.wait()
    moments = [jnp.zeros((8, 128), jnp.float32) for _ in range(6)]
    for j in range(CHUNKS):
        get_halo(0, j)
        span = slice(j * width, (j + 1) * width)
        cond = here(0, j)
        diagonal = None
        for i, name in enumerate(names):
            face = cond + near(0, j, name)
            coefs[i, :, span] = face
            diagonal = face if diagonal is None else diagonal + face
        inverse = 1.0 / diagonal
        inv_ref[:, span] = inverse
        source = src_ref[:, span]
        field = source * inverse
        put_field(1, j, field)
        send_field(1, j)
        moments[0] = moments[0] + fold(field * source)
    for stage in (1, 2):
        for j in range(CHUNKS):
            get_halo(stage, j)
            span = slice(j * width, (j + 1) * width)
            image = None
            for i, name in enumerate(names):
                term = coefs[i, :, span] * near(stage, j, name)
                image = term if image is None else image + term
            field = inv_ref[:, span] * image
            put_field(stage + 1, j, field)
            send_field(stage + 1, j)
            moments[2 * stage - 1] = moments[2 * stage - 1] + fold(here(stage, j) * image)
            moments[2 * stage] = moments[2 * stage] + fold(field * image)
        deliver(stage - 1)
    for j in range(CHUNKS):
        get_halo(3, j)
        span = slice(j * width, (j + 1) * width)
        side = "below" if j < CHUNKS // 2 else "above"
        image = None
        for name in ("west", "north", side):
            term = coefs[names.index(name), :, span] * near(3, j, name)
            image = term if image is None else image + term
        moments[5] = moments[5] + fold(here(3, j) * image)
    moments[5] = 2.0 * moments[5]

    own_sums = jnp.zeros((1, 128), jnp.float32)
    place = lax.broadcasted_iota(jnp.int32, (1, 128), 1)
    for k in range(6):
        own = jnp.sum(jnp.sum(moments[k], axis=0, keepdims=True), axis=1, keepdims=True)
        own_sums = jnp.where(place == k, own, own_sums)
    sums[layer * n_slab + slab] = own_sums
    repeat(1, n_layer * n_slab, lambda n: sum_copy(n).start())
    deliver(2)
    for stage in range(4):
        for j in range(CHUNKS):
            for direction in range(4):
                if sent_with(stage, direction, j):

                    @pl.when(sends_to[direction] & wanted(stage, direction, j, layer))
                    def _():
                        halo_copy(stage, direction, j).wait_send()
    for k in range(ITERS - 1):
        repeat(1, n_pair * n_slab, lambda n: tile_copy(k, n).wait_recv())
        repeat(1, n_pair * n_slab, lambda n: tile_copy(k, n).wait_send())
    all_sums.wait_recv()
    total = jnp.sum(sums[...], axis=0)
    scales = [2.0 * c for c in cg_coefficients([total[:, k : k + 1] for k in range(6)])]

    for j in range(CHUNKS):
        value = scales[0] * here(1, j) + scales[1] * here(2, j) + scales[2] * here(3, j)
        x_buf[:, j * width : (j + 1) * width] = value
    x_copy = pltpu.make_async_copy(x_buf, x_out.at[0], local_sem.at[0])
    x_copy.start()

    repeat(1, n_pair * n_slab, lambda n: tile_copy(ITERS - 1, n).wait_recv())

    def combine(i):
        value = None
        for k in range(ITERS):
            term = scales[k] * sum(tile_recv[k, p, i] for p in range(n_pair))
            value = term if value is None else value + term
        tiles[i] = value

    repeat(0, n_slab, combine)
    if tile_rows == 1:
        turned = jnp.transpose(tiles[...].reshape(TILE, TILE))
        for k in range(owned_count):
            g_buf[k] = turned[k * strip : (k + 1) * strip]
    else:
        count = jnp.int32(0)
        picked = [jnp.int32(0)] * owned_count
        for r in range(tile_rows):
            for t in range(tiles_across):
                mine = owner_ref[r, t] == slab
                picked = [jnp.where(mine & (count == k), r, p) for k, p in enumerate(picked)]
                count = jnp.where(mine, count + 1, count)
        for k in range(owned_count):
            block = tiles[pl.ds(picked[k] * per_tile, per_tile)].reshape(TILE, TILE)
            g_buf[k] = jnp.transpose(block)[0:strip]

    g_copy = pltpu.make_async_copy(g_buf, g_out, local_sem.at[1])
    g_copy.start()

    all_sums.wait_send()
    repeat(1, n_pair * n_slab, lambda n: tile_copy(ITERS - 1, n).wait_send())
    x_copy.wait()
    g_copy.wait()


def per_device(adjoint_source, conductivity, tile_owner):
    n_slab, n_layer = lax.axis_size("slab"), lax.axis_size("layer")
    depth, rows, cols = adjoint_source.shape
    owned = tile_owner.shape[0] * tile_owner.shape[1] // n_slab
    strip = TILE // n_layer
    width = cols // CHUNKS
    f32 = jnp.float32
    return pl.pallas_call(
        functools.partial(kernel, n_slab, n_layer),
        out_shape=(
            jax.ShapeDtypeStruct((depth, rows, cols), f32),
            jax.ShapeDtypeStruct((owned, strip, TILE), f32),
        ),
        in_specs=[pl.BlockSpec(memory_space=pltpu.HBM)] * 3,
        out_specs=(pl.BlockSpec(memory_space=pl.ANY), pl.BlockSpec(memory_space=pl.ANY)),
        scratch_shapes=[
            pltpu.VMEM((rows, cols), f32),
            pltpu.SMEM(tile_owner.shape, jnp.int32),
            pltpu.VMEM((4, rows + 16, cols + 2 * PAD), f32),
            pltpu.VMEM((6, rows, cols), f32),
            pltpu.VMEM((rows, cols), f32),
            pltpu.VMEM((4, 2, rows, cols), f32),
            pltpu.VMEM((4, 2, ROW_CHUNKS, 1, cols // ROW_CHUNKS), f32),
            pltpu.VMEM((4, 2, ROW_CHUNKS, 1, cols // ROW_CHUNKS), f32),
            pltpu.VMEM((n_layer * n_slab, 1, 128), f32),
            pltpu.VMEM((rows, cols), f32),
            pltpu.VMEM((cols // TILE, rows, TILE), f32),
            pltpu.VMEM((ITERS, n_layer // 2, n_slab, rows, TILE), f32),
            pltpu.VMEM((ITERS, n_layer // 2, n_slab, rows, TILE), f32),
            pltpu.VMEM((n_slab, rows, TILE), f32),
            pltpu.VMEM((owned, strip, TILE), f32),
            pltpu.SMEM((n_slab,), jnp.int32),
            pltpu.SemaphoreType.DMA((4, 4, CHUNKS)),
            pltpu.SemaphoreType.DMA((4, 4, CHUNKS)),
            pltpu.SemaphoreType.DMA,
            pltpu.SemaphoreType.DMA,
            pltpu.SemaphoreType.DMA((ITERS, n_layer // 2 * n_slab)),
            pltpu.SemaphoreType.DMA((ITERS, n_layer // 2 * n_slab)),
            pltpu.SemaphoreType.DMA((3,)),
        ],
        compiler_params=pltpu.CompilerParams(
            collective_id=0, has_side_effects=True, vmem_limit_bytes=48 * 1024 * 1024
        ),
        name="stack_cg",
    )(*[pltpu.with_memory_space_constraint(v, pltpu.HBM) for v in (adjoint_source, conductivity, tile_owner)])


def solution(mesh):
    placed = (P("layer", "slab", None), P("layer", "slab", None), P())
    return jax.shard_map(
        per_device,
        mesh=mesh,
        in_specs=placed,
        out_specs=(P("layer", "slab", None), P("slab", "layer", None)),
        check_vma=False,
    )
```

```python
import functools

import jax
import jax.numpy as jnp
from jax import lax
from jax.experimental import pallas as pl
from jax.experimental.pallas import tpu as pltpu
from jax.sharding import PartitionSpec as P

TILE = 128
ITERS = 3
CHUNKS = 4
ROW_CHUNKS = 2
PAD = 128
MESH = pl.DeviceIdType.MESH


def fold(value):
    rows = sum(value[i : i + 8] for i in range(0, value.shape[0], 8))
    return sum(rows[:, i : i + 128] for i in range(0, value.shape[1], 128))


def cg_coefficients(mu):
    def inner(a, b):
        total = None
        for k in range(len(a) + len(b) - 1):
            coef = None
            for i in range(len(a)):
                if 0 <= k - i < len(b):
                    term = a[i] * b[k - i]
                    coef = term if coef is None else coef + term
            total = coef * mu[k] if total is None else total + coef * mu[k]
        return total

    def axpy(a, s, b):
        out = []
        for i in range(max(len(a), len(b))):
            if i >= len(b):
                out.append(a[i])
            elif i >= len(a):
                out.append(s * b[i])
            else:
                out.append(a[i] + s * b[i])
        return out

    one = jnp.ones_like(mu[0])
    zero = jnp.zeros_like(mu[0])
    sol, res, direction, now = [zero], [one], [one], mu[0]
    for iteration in range(ITERS):
        image = axpy(direction + [zero], -one, [zero] + direction)
        step = now / inner(direction, image)
        sol = axpy(sol, step, direction)
        if iteration + 1 < ITERS:
            res = axpy(res, -step, image)
            new = inner(res, res)
            direction = axpy(res, new / now, direction)
            now = new
    return sol


def kernel(
    n_slab,
    n_layer,
    src_hbm,
    cond_hbm,
    owner_hbm,
    x_out,
    g_out,
    src_ref,
    owner_ref,
    fields,
    coefs,
    inv_ref,
    layer_halo,
    row_send,
    row_recv,
    sums,
    x_buf,
    x_tiles,
    tile_send,
    tile_recv,
    tiles,
    g_buf,
    table,
    halo_ssem,
    halo_rsem,
    sum_ssem,
    sum_rsem,
    tile_ssem,
    tile_rsem,
    local_sem,
):
    slab = lax.axis_index("slab")
    layer = lax.axis_index("layer")
    rows, cols = src_ref.shape
    width = cols // CHUNKS
    per_row = CHUNKS // ROW_CHUNKS
    top, bottom = 8, 8 + rows
    tile_rows, tiles_across = owner_ref.shape
    strip = TILE // n_layer
    capacity = max(1, tiles_across // n_slab)
    owned_count = g_out.shape[0]
    per_tile = TILE // rows

    pair, core = layer // 2, layer % 2
    n_pair = n_layer // 2

    def turn(me, d, count):
        return lax.rem(me + d, count)

    def any_peer(n):
        return {"layer": turn(layer, n // n_slab, n_layer), "slab": turn(slab, n % n_slab, n_slab)}

    def tile_peer(n):
        to_pair, to_slab = turn(pair, n // n_slab, n_pair), turn(slab, n % n_slab, n_slab)
        return to_pair, to_slab, {"layer": 2 * to_pair + core, "slab": to_slab}

    def repeat(start, stop, body):
        if stop - start <= 32:
            for n in range(start, stop):
                body(n)
        else:
            lax.fori_loop(start, stop, lambda n, carry: (body(n), carry)[1], 0)

    barrier = pltpu.get_barrier_semaphore()

    def greet(device):
        pl.semaphore_signal(barrier, inc=1, device_id=device, device_id_type=MESH)

    n_greet = n_layer * n_slab - 1
    repeat(1, n_greet + 1, lambda n: greet(any_peer(n)))

    cond_copy = pltpu.make_async_copy(
        cond_hbm.at[0], fields.at[0, pl.ds(top, rows), pl.ds(PAD, cols)], local_sem.at[0]
    )
    src_copy = pltpu.make_async_copy(src_hbm.at[0], src_ref, local_sem.at[1])
    owner_copy = pltpu.make_async_copy(owner_hbm, owner_ref, local_sem.at[2])
    cond_copy.start()
    src_copy.start()
    owner_copy.start()

    for s in range(4):
        fields[s, :, 0:PAD] = jnp.zeros((rows + 16, PAD), jnp.float32)
        fields[s, :, PAD + cols :] = jnp.zeros((rows + 16, PAD), jnp.float32)
    for d, axis_end in enumerate((layer == 0, layer == n_layer - 1)):

        @pl.when(axis_end)
        def _():
            for s in range(4):
                layer_halo[s, d] = jnp.zeros((rows, cols), jnp.float32)

    for d, axis_end in enumerate((slab == 0, slab == n_slab - 1)):

        @pl.when(axis_end)
        def _():
            for s in range(4):
                for j in range(ROW_CHUNKS):
                    row_recv[s, d, j] = jnp.zeros((1, cols // ROW_CHUNKS), jnp.float32)

    sends_to = (layer < n_layer - 1, layer > 0, slab < n_slab - 1, slab > 0)
    gets_from = (layer > 0, layer < n_layer - 1, slab > 0, slab < n_slab - 1)
    target = (
        {"layer": lax.rem(layer + 1, n_layer)},
        {"layer": lax.rem(layer + n_layer - 1, n_layer)},
        {"slab": lax.rem(slab + 1, n_slab)},
        {"slab": lax.rem(slab + n_slab - 1, n_slab)},
    )

    def used(stage, direction, j):
        if stage < 3:
            return True
        return direction < 3

    def wanted(stage, direction, j, sender_layer):
        if stage == 3 and direction == 0 and j >= CHUNKS // 2:
            return sender_layer % 2 == 0
        if stage == 3 and direction == 1 and j < CHUNKS // 2:
            return sender_layer % 2 == 1
        return True

    def halo_copy(stage, direction, j):
        span = pl.ds(j * width, width)
        slot = j if direction < 2 else j // per_row
        if direction < 2:
            source = fields.at[stage, pl.ds(top, rows), pl.ds(PAD + j * width, width)]
            dest = layer_halo.at[stage, direction, :, span]
        else:
            source = row_send.at[stage, direction - 2, j // per_row]
            dest = row_recv.at[stage, direction - 2, j // per_row]
        return pltpu.make_async_remote_copy(
            src_ref=source,
            dst_ref=dest,
            send_sem=halo_ssem.at[stage, direction, slot],
            recv_sem=halo_rsem.at[stage, direction, slot],
            device_id=target[direction],
            device_id_type=MESH,
        )

    def put_field(stage, j, value):
        fields[stage, top:bottom, PAD + j * width : PAD + (j + 1) * width] = value
        part = slice((j % per_row) * width, (j % per_row + 1) * width)
        row_send[stage, 0, j // per_row, :, part] = value[rows - 1 : rows]
        row_send[stage, 1, j // per_row, :, part] = value[0:1]

    def sent_with(stage, direction, j):
        return used(stage, direction, j) and (direction < 2 or j % per_row == per_row - 1)

    def got_with(stage, direction, j):
        return used(stage, direction, j) and (direction < 2 or j % per_row == 0)

    def send_field(stage, j):
        for direction in range(4):
            if sent_with(stage, direction, j):

                @pl.when(sends_to[direction] & wanted(stage, direction, j, layer))
                def _():
                    halo_copy(stage, direction, j).start()

    def get_halo(stage, j):
        for direction in range(4):
            if got_with(stage, direction, j):

                @pl.when(gets_from[direction] & wanted(stage, direction, j, layer + 1))
                def _():
                    halo_copy(stage, direction, j).wait_recv()

        span = slice(PAD + j * width, PAD + (j + 1) * width)
        part = slice((j % per_row) * width, (j % per_row + 1) * width)
        fields[stage, top - 1 : top, span] = row_recv[stage, 0, j // per_row, :, part]
        if stage < 3:
            fields[stage, bottom : bottom + 1, span] = row_recv[stage, 1, j // per_row, :, part]

    def near(stage, j, which):
        c0 = j * width
        if which == "west":
            ext = fields[stage, top:bottom, c0 : c0 + width + 2 * PAD]
            return pltpu.roll(ext, 1, 1)[:, PAD : PAD + width]
        if which == "east":
            ext = fields[stage, top:bottom, c0 : c0 + width + 2 * PAD]
            return pltpu.roll(ext, width + 2 * PAD - 1, 1)[:, PAD : PAD + width]
        span = slice(PAD + c0, PAD + c0 + width)
        if which == "north":
            return fields[stage, top - 1 : bottom - 1, span]
        if which == "south":
            return fields[stage, top + 1 : bottom + 1, span]
        return layer_halo[stage, 0 if which == "below" else 1, :, c0 : c0 + width]

    names = ("west", "east", "north", "south", "below", "above")

    def here(stage, j):
        return fields[stage, top:bottom, PAD + j * width : PAD + (j + 1) * width]

    cond_copy.wait()
    for j in range(CHUNKS):
        part = slice((j % per_row) * width, (j % per_row + 1) * width)
        span = slice(PAD + j * width, PAD + (j + 1) * width)
        row_send[0, 0, j // per_row, :, part] = fields[0, bottom - 1 : bottom, span]
        row_send[0, 1, j // per_row, :, part] = fields[0, top : top + 1, span]
    pl.semaphore_wait(barrier, n_greet)
    for j in range(CHUNKS):
        send_field(0, j)

    owner_copy.wait()
    my_row = slab // per_tile

    def list_tiles(owner, carry):
        packed = jnp.int32(0)
        for t in range(tiles_across):
            packed = jnp.where(owner_ref[my_row, t] == owner, packed * 256 + t, packed)
        table[owner] = packed
        return carry

    lax.fori_loop(0, n_slab, list_tiles, 0)

    def sum_copy(n):
        return pltpu.make_async_remote_copy(
            src_ref=sums.at[layer * n_slab + slab],
            dst_ref=sums.at[layer * n_slab + slab],
            send_sem=sum_ssem,
            recv_sem=sum_rsem,
            device_id=any_peer(n),
            device_id_type=MESH,
        )

    others = pl.ds(0, n_layer * n_slab - 1)
    all_sums = pltpu.make_async_remote_copy(
        src_ref=sums.at[others],
        dst_ref=sums.at[others],
        send_sem=sum_ssem,
        recv_sem=sum_rsem,
        device_id=any_peer(1),
        device_id_type=MESH,
    )

    def all_tiles(k):
        other_tiles = pl.ds(0, n_pair * n_slab - 1)
        return pltpu.make_async_remote_copy(
            src_ref=tile_send.at[k, other_tiles],
            dst_ref=tile_recv.at[k, other_tiles],
            send_sem=tile_ssem.at[k],
            recv_sem=tile_rsem.at[k],
            device_id=tile_peer(1)[2],
            device_id_type=MESH,
        )

    def tile_copy(k, n):
        to_pair, to_slab, device = tile_peer(n)
        return pltpu.make_async_remote_copy(
            src_ref=tile_send.at[k, to_pair * n_slab + to_slab],
            dst_ref=tile_recv.at[k, pair * n_slab + slab],
            send_sem=tile_ssem.at[k],
            recv_sem=tile_rsem.at[k],
            device_id=device,
            device_id_type=MESH,
        )

    lane = lax.broadcasted_iota(jnp.int32, (rows, TILE), 1) // strip

    def deliver(k):
        for j in range(CHUNKS):
            value = here(k + 1, j) + layer_halo[k + 1, 1 - core, :, j * width : (j + 1) * width]
            for t in range(width // TILE):
                x_tiles[j * (width // TILE) + t] = value[:, t * TILE : (t + 1) * TILE]

        def pack(owner):
            packed = table[owner]
            pieces = [None] * n_pair
            for q in range(capacity):
                t = lax.shift_right_logical(packed, 8 * (capacity - 1 - q)) & 255
                tile = x_tiles[t]
                tile = jnp.where(core == 1, pltpu.roll(tile, TILE - strip, 1), tile)
                for p in range(n_pair):
                    shift = ((q - 2 * p) * strip) % TILE
                    moved = tile if shift == 0 else pltpu.roll(tile, shift, 1)
                    pieces[p] = moved if q == 0 else jnp.where(lane == q, moved, pieces[p])
            for p in range(n_pair):
                tile_send[k, p * n_slab + owner] = pieces[p]

        repeat(0, n_slab, pack)
        repeat(1, n_pair * n_slab, lambda n: tile_copy(k, n).start())
        tile_recv[k, pair * n_slab + slab] = tile_send[k, pair * n_slab + slab]

    src_copy.wait()
    moments = [jnp.zeros((8, 128), jnp.float32) for _ in range(6)]
    for j in range(CHUNKS):
        get_halo(0, j)
        span = slice(j * width, (j + 1) * width)
        cond = here(0, j)
        diagonal = None
        for i, name in enumerate(names):
            face = cond + near(0, j, name)
            coefs[i, :, span] = face
            diagonal = face if diagonal is None else diagonal + face
        inverse = 1.0 / diagonal
        inv_ref[:, span] = inverse
        source = src_ref[:, span]
        field = source * inverse
        put_field(1, j, field)
        send_field(1, j)
        moments[0] = moments[0] + fold(field * source)
    for stage in (1, 2):
        for j in range(CHUNKS):
            get_halo(stage, j)
            span = slice(j * width, (j + 1) * width)
            image = None
            for i, name in enumerate(names):
                term = coefs[i, :, span] * near(stage, j, name)
                image = term if image is None else image + term
            field = inv_ref[:, span] * image
            put_field(stage + 1, j, field)
            send_field(stage + 1, j)
            moments[2 * stage - 1] = moments[2 * stage - 1] + fold(here(stage, j) * image)
            moments[2 * stage] = moments[2 * stage] + fold(field * image)
        deliver(stage - 1)
    for j in range(CHUNKS):
        get_halo(3, j)
        span = slice(j * width, (j + 1) * width)
        side = "below" if j < CHUNKS // 2 else "above"
        image = None
        for name in ("west", "north", side):
            term = coefs[names.index(name), :, span] * near(3, j, name)
            image = term if image is None else image + term
        moments[5] = moments[5] + fold(here(3, j) * image)
    moments[5] = 2.0 * moments[5]

    own_sums = jnp.zeros((1, 128), jnp.float32)
    place = lax.broadcasted_iota(jnp.int32, (1, 128), 1)
    for k in range(6):
        own = jnp.sum(jnp.sum(moments[k], axis=0, keepdims=True), axis=1, keepdims=True)
        own_sums = jnp.where(place == k, own, own_sums)
    sums[layer * n_slab + slab] = own_sums
    repeat(1, n_layer * n_slab, lambda n: sum_copy(n).start())
    deliver(2)
    for stage in range(4):
        for j in range(CHUNKS):
            for direction in range(4):
                if sent_with(stage, direction, j):

                    @pl.when(sends_to[direction] & wanted(stage, direction, j, layer))
                    def _():
                        halo_copy(stage, direction, j).wait_send()
    for k in range(ITERS - 1):
        all_tiles(k).wait_recv()
        all_tiles(k).wait_send()
    all_sums.wait_recv()
    total = jnp.sum(sums[...], axis=0)
    scales = [2.0 * c for c in cg_coefficients([total[:, k : k + 1] for k in range(6)])]

    for j in range(CHUNKS):
        value = scales[0] * here(1, j) + scales[1] * here(2, j) + scales[2] * here(3, j)
        x_buf[:, j * width : (j + 1) * width] = value
    x_copy = pltpu.make_async_copy(x_buf, x_out.at[0], local_sem.at[0])
    x_copy.start()

    all_tiles(ITERS - 1).wait_recv()

    def combine(i):
        value = None
        for k in range(ITERS):
            term = scales[k] * sum(tile_recv[k, p * n_slab + i] for p in range(n_pair))
            value = term if value is None else value + term
        tiles[i] = value

    repeat(0, n_slab, combine)
    if tile_rows == 1:
        turned = jnp.transpose(tiles[...].reshape(TILE, TILE))
        for k in range(owned_count):
            g_buf[k] = turned[k * strip : (k + 1) * strip]
    else:
        count = jnp.int32(0)
        picked = [jnp.int32(0)] * owned_count
        for r in range(tile_rows):
            for t in range(tiles_across):
                mine = owner_ref[r, t] == slab
                picked = [jnp.where(mine & (count == k), r, p) for k, p in enumerate(picked)]
                count = jnp.where(mine, count + 1, count)
        for k in range(owned_count):
            block = tiles[pl.ds(picked[k] * per_tile, per_tile)].reshape(TILE, TILE)
            g_buf[k] = jnp.transpose(block)[0:strip]

    g_copy = pltpu.make_async_copy(g_buf, g_out, local_sem.at[1])
    g_copy.start()

    all_sums.wait_send()
    all_tiles(ITERS - 1).wait_send()
    x_copy.wait()
    g_copy.wait()


def per_device(adjoint_source, conductivity, tile_owner):
    n_slab, n_layer = lax.axis_size("slab"), lax.axis_size("layer")
    depth, rows, cols = adjoint_source.shape
    owned = tile_owner.shape[0] * tile_owner.shape[1] // n_slab
    strip = TILE // n_layer
    width = cols // CHUNKS
    f32 = jnp.float32
    return pl.pallas_call(
        functools.partial(kernel, n_slab, n_layer),
        out_shape=(
            jax.ShapeDtypeStruct((depth, rows, cols), f32),
            jax.ShapeDtypeStruct((owned, strip, TILE), f32),
        ),
        in_specs=[pl.BlockSpec(memory_space=pltpu.HBM)] * 3,
        out_specs=(pl.BlockSpec(memory_space=pl.ANY), pl.BlockSpec(memory_space=pl.ANY)),
        scratch_shapes=[
            pltpu.VMEM((rows, cols), f32),
            pltpu.SMEM(tile_owner.shape, jnp.int32),
            pltpu.VMEM((4, rows + 16, cols + 2 * PAD), f32),
            pltpu.VMEM((6, rows, cols), f32),
            pltpu.VMEM((rows, cols), f32),
            pltpu.VMEM((4, 2, rows, cols), f32),
            pltpu.VMEM((4, 2, ROW_CHUNKS, 1, cols // ROW_CHUNKS), f32),
            pltpu.VMEM((4, 2, ROW_CHUNKS, 1, cols // ROW_CHUNKS), f32),
            pltpu.VMEM((n_layer * n_slab, 1, 128), f32),
            pltpu.VMEM((rows, cols), f32),
            pltpu.VMEM((cols // TILE, rows, TILE), f32),
            pltpu.VMEM((ITERS, n_layer // 2 * n_slab, rows, TILE), f32),
            pltpu.VMEM((ITERS, n_layer // 2 * n_slab, rows, TILE), f32),
            pltpu.VMEM((n_slab, rows, TILE), f32),
            pltpu.VMEM((owned, strip, TILE), f32),
            pltpu.SMEM((n_slab,), jnp.int32),
            pltpu.SemaphoreType.DMA((4, 4, CHUNKS)),
            pltpu.SemaphoreType.DMA((4, 4, CHUNKS)),
            pltpu.SemaphoreType.DMA,
            pltpu.SemaphoreType.DMA,
            pltpu.SemaphoreType.DMA((ITERS,)),
            pltpu.SemaphoreType.DMA((ITERS,)),
            pltpu.SemaphoreType.DMA((3,)),
        ],
        compiler_params=pltpu.CompilerParams(
            collective_id=0, has_side_effects=True, vmem_limit_bytes=48 * 1024 * 1024
        ),
        name="stack_cg",
    )(*[pltpu.with_memory_space_constraint(v, pltpu.HBM) for v in (adjoint_source, conductivity, tile_owner)])


def solution(mesh):
    placed = (P("layer", "slab", None), P("layer", "slab", None), P())
    return jax.shard_map(
        per_device,
        mesh=mesh,
        in_specs=placed,
        out_specs=(P("layer", "slab", None), P("slab", "layer", None)),
        check_vma=False,
    )
```
